32 devices in a mesh: row: 8 (over y, x, core), col: 4 (over z).
Axes of the slice: x: 2, y: 2, z: 4, core: 2. Of those that a mesh axis runs over, the one named last changes fastest.
Arguments:
- pair_cc: bfloat16 [2, 2048, 6144], P(None, 'row', 'col'), may hold values from -6 to 6
- screened: bfloat16 [2, 6144, 6144], P(None, 'row', 'col'), may hold values from -0.078125 to 0.078125
- pair_vv: bfloat16 [2, 512, 6144], P(None, 'col', 'row'), may hold values from -0.078125 to 0.078125
Outputs:
- kernel: float32 [2, 2048, 512], P(None, 'row', 'col')
The draws below stay inside these ranges and needn't reach their ends.
All inputs are finite; a program needn't handle non-finite values.
Results may differ from the reference program's by a relative error of at most 0.0003.
Values may be sent and summed in bfloat16 or wider, within the bound.
No kernel may reach another device: no remote copies, remote signals or barrier semaphores. Data moves between devices by JAX's collectives and lax.ppermute only.
A program may use at most 64 MiB of HBM per device.

```python
import jax
import jax.numpy as jnp
from jax import lax

NG = 6144
PC = 2048
PV = 512


def block_scale(rng, extent, pieces, low, top_value):
    gain, own = 1.0, jax.random.fold_in(rng, 6)
    for dim, shards_of in pieces:
        steps = jnp.exp(jax.random.uniform(jax.random.fold_in(own, dim), (shards_of,), jnp.float32, low / len(pieces), top_value / len(pieces)))
        gain = gain * jnp.repeat(steps, extent[dim] // shards_of).reshape([-1 if axis == dim else 1 for axis in range(len(extent))])
    return gain


def noise(key, extent, deviation, bound, split=(), dtype=jnp.bfloat16):
    factor_of = block_scale(key, extent, split, -0.22, 0.18) if split else 1.0
    result = jax.random.normal(key, extent, jnp.float32) * deviation * factor_of
    return jnp.minimum(jnp.maximum(result, -bound), bound).astype(dtype)


def setup_inputs(seed: int = 0) -> dict:
    arg_keys = jax.random.split(jax.random.key(seed), 4)
    return {
        "pair_cc": noise(arg_keys[0], (2, PC, NG), 1.0, 6.0, ((1, 8), (2, 4))),
        "screened": noise(arg_keys[1], (2, NG, NG), NG ** -0.5, 0.078125, ((1, 8), (2, 4))),
        "pair_vv": noise(arg_keys[2], (2, PV, NG), NG ** -0.5, 0.078125, ((1, 4), (2, 8))),
    }


def product_nt(left, right):
    return lax.dot_general(left, right, (((1,), (1,)), ((), ())), preferred_element_type=jnp.float32)


def split_parts(values):
    upper = values.astype(jnp.bfloat16)
    lower = (values - upper.astype(jnp.float32)).astype(jnp.bfloat16)
    return upper, lower


def mixed_nn(data, inter):
    upper, lower = split_parts(inter)
    return jnp.dot(data, upper, preferred_element_type=jnp.float32) + jnp.dot(data, lower, preferred_element_type=jnp.float32)


def reference(pair_cc, screened, pair_vv):
    inner_re = product_nt(screened[0], pair_vv[0]) - product_nt(screened[1], pair_vv[1])
    inner_im = product_nt(screened[0], pair_vv[1]) + product_nt(screened[1], pair_vv[0])
    kernel_re = mixed_nn(pair_cc[0], inner_re) + mixed_nn(pair_cc[1], inner_im)
    kernel_im = mixed_nn(pair_cc[0], inner_im) - mixed_nn(pair_cc[1], inner_re)
    return jnp.stack([kernel_re, kernel_im])
```

```python
import functools

import jax
import jax.numpy as jnp
from jax import lax
from jax.experimental import pallas as pl
from jax.experimental.pallas import tpu as pltpu
from jax.sharding import PartitionSpec as P

LANES = 128
HEAD = 16
SPAN = 126.0
CHUNKS = 2
BF = jnp.bfloat16
F32 = jnp.float32


def half_nt(left, right):
    return lax.dot_general(
        left, right, (((1,), (1,)), ((), ())), preferred_element_type=jnp.float32
    )


def split_parts(values):
    upper = values.astype(jnp.bfloat16)
    lower = (values - upper.astype(jnp.float32)).astype(jnp.bfloat16)
    return (upper, lower)


def mixed_nn(data, inter):
    upper, lower = split_parts(inter)
    return jnp.dot(data, upper, preferred_element_type=jnp.float32) + jnp.dot(
        data, lower, preferred_element_type=jnp.float32
    )


def gathered(pair_cc, screened, pair_vv):
    cc_whole = lax.all_gather(pair_cc, "col", axis=2, tiled=True)
    vv_whole = lax.all_gather(pair_vv, "row", axis=2, tiled=True)
    piece = lax.all_gather(screened, "col", axis=2, tiled=True)
    inner_re = half_nt(piece[0], vv_whole[0]) - half_nt(piece[1], vv_whole[1])
    inner_im = half_nt(piece[0], vv_whole[1]) + half_nt(piece[1], vv_whole[0])
    right_block = jnp.stack([inner_re, inner_im])
    piece = lax.all_gather(right_block, "row", axis=1, tiled=True)
    out_re = mixed_nn(cc_whole[0], piece[0]) + mixed_nn(cc_whole[1], piece[1])
    out_im = mixed_nn(cc_whole[0], piece[1]) - mixed_nn(cc_whole[1], piece[0])
    return jnp.stack([out_re, out_im])


def bound_of(top):
    top = jnp.max(top, axis=(0, 1), keepdims=True)
    top = jnp.maximum(top, 1e-30) * (1.0 + 2.0**-7)
    return top.astype(BF).astype(F32)


def fold_top(values):
    return jnp.max(jnp.abs(values).reshape(-1, 8, LANES), axis=0)


def code(values, bound):
    return jnp.exp2(values * (SPAN / bound)).astype(BF)


def decode(coded, bound):
    return jnp.log2(coded.astype(F32)) * (bound * (1.0 / SPAN))


def head_of(ref):
    return ref[0:1, :].astype(F32)


def put_head(ref, bound):
    ref[0:HEAD, :] = jnp.broadcast_to(bound, (HEAD, LANES)).astype(BF)


def call(body, outs, scratch, name, args, flops=0):
    nbytes = sum(a.size * a.dtype.itemsize for a in args) + sum(
        functools.reduce(lambda p, q: p * q, o.shape) * o.dtype.itemsize for o in outs
    )
    specs = [pl.BlockSpec(memory_space=pltpu.SMEM)] + [
        pl.BlockSpec(memory_space=pltpu.VMEM)
    ] * (len(args) - 1)
    return pl.pallas_call(
        body,
        out_shape=outs,
        in_specs=specs,
        out_specs=[pl.BlockSpec(memory_space=pltpu.VMEM)] * len(outs),
        scratch_shapes=scratch,
        compiler_params=pltpu.CompilerParams(vmem_limit_bytes=48 * 1024 * 1024),
        cost_estimate=pl.CostEstimate(
            flops=flops, bytes_accessed=nbytes, transcendentals=0
        ),
        name=name,
    )(*args)


def route_body(parts, where_ref, *refs):
    ins, outs = refs[:parts], refs[parts:]
    m = where_ref[3]
    for v in range(parts):

        @pl.when(m == v)
        def _(v=v):
            for d in range(parts):
                outs[d][...] = ins[v ^ d][...]


def inner_body(parts, cores, rows, where_ref, w_ref, *refs):
    n_in = parts * cores
    ins, outs = refs[:n_in], refs[n_in : n_in + parts]
    x_ref, t_ref = refs[n_in + parts :]
    width = ins[0].shape[1]
    core = where_ref[1]
    group = ins[0].shape[0]
    for c in range(cores):
        at = pl.multiple_of((core ^ c) * width, LANES)
        for i in range(parts):
            x_ref[i * group : (i + 1) * group, pl.ds(at, width)] = ins[
                c * parts + i
            ][...]
    n_g = w_ref.shape[1]
    tops = [jnp.zeros((8, LANES), F32) for _ in range(parts)]
    tile = 256
    for g in range(0, n_g, tile):
        with_re = half_nt(x_ref[...], w_ref[0, g : g + tile, :])
        with_im = half_nt(x_ref[...], w_ref[1, g : g + tile, :])
        with_re = with_re.reshape(-1, 2, rows, tile)
        with_im = with_im.reshape(-1, 2, rows, tile)
        t_re = with_re[:, 0] - with_im[:, 1]
        t_im = with_im[:, 0] + with_re[:, 1]
        both = jnp.stack([t_re, t_im], axis=1).reshape(-1, tile)
        for i in range(parts):
            mine = both[i * group : (i + 1) * group]
            for l in range(0, tile, LANES):
                block = mine[:, l : l + LANES]
                tops[i] = jnp.maximum(tops[i], fold_top(block))
                t_ref[i, (g + l) // LANES] = block
    for i in range(parts):
        bound = bound_of(tops[i])
        put_head(outs[i], bound)
        for l in range(n_g // LANES):
            at = HEAD + l * group
            outs[i][at : at + group, :] = code(t_ref[i, l], bound)


def sum_body(parts, where_ref, *refs):
    ins, out = refs[:parts], refs[parts]
    t_ref = refs[parts + 1]
    n_l, group = t_ref.shape[0], t_ref.shape[1]
    step = group // parts
    top = jnp.zeros((8, LANES), F32)
    bounds = [head_of(ins[d]) for d in range(parts)]
    for l in range(n_l):
        for s in range(parts):
            total = None
            for d in range(parts):
                at = HEAD + l * group + (s ^ d) * step
                term = decode(ins[d][at : at + step, :], bounds[d])
                total = term if total is None else total + term
            top = jnp.maximum(top, fold_top(total))
            t_ref[l, s * step : (s + 1) * step, :] = total
    bound = bound_of(top)
    put_head(out, bound)
    for l in range(n_l):
        at = HEAD + l * group
        out[at : at + group, :] = code(t_ref[l], bound)


def outer_body(parts, cores, rows, where_ref, a_ref, *refs):
    n_in = parts * cores
    ins, outs = refs[:n_in], refs[n_in : n_in + parts]
    hi_ref, lo_ref = refs[n_in + parts :]
    core = where_ref[1]
    n_k = hi_ref.shape[1]
    width = n_k // cores
    group = (ins[0].shape[0] - HEAD) // (width // LANES)
    for c in range(cores):
        for i in range(parts):
            ref = ins[c * parts + i]
            bound = head_of(ref)
            for l in range(width // LANES):
                at = HEAD + l * group
                values = decode(ref[at : at + group, :], bound)
                upper, lower = split_parts(values)
                lane = pl.multiple_of((core ^ c) * width + l * LANES, LANES)
                hi_ref[i * group : (i + 1) * group, pl.ds(lane, LANES)] = upper
                lo_ref[i * group : (i + 1) * group, pl.ds(lane, LANES)] = lower
    n_p = a_ref.shape[1]
    with_re = half_nt(hi_ref[...], a_ref[0]) + half_nt(lo_ref[...], a_ref[0])
    with_im = half_nt(hi_ref[...], a_ref[1]) + half_nt(lo_ref[...], a_ref[1])
    with_re = with_re.reshape(parts, parts, 2, rows, n_p)
    with_im = with_im.reshape(parts, parts, 2, rows, n_p)
    k_re = with_re[:, :, 0] + with_im[:, :, 1]
    k_im = with_re[:, :, 1] - with_im[:, :, 0]
    for d in range(parts):
        both = jnp.stack([k_re[:, d], k_im[:, d]], axis=1).reshape(-1, n_p)
        if d == 0:
            outs[0][...] = both
            continue
        top = jnp.zeros((8, LANES), F32)
        for l in range(0, n_p, LANES):
            top = jnp.maximum(top, fold_top(both[:, l : l + LANES]))
        bound = bound_of(top)
        put_head(outs[d], bound)
        n_r = both.shape[0]
        for l in range(n_p // LANES):
            at = HEAD + l * n_r
            outs[d][at : at + n_r, :] = code(both[:, l * LANES : (l + 1) * LANES], bound)


def last_body(parts, chunks, rows, where_ref, *refs):
    ins, out = refs[: parts * chunks], refs[parts * chunks]
    k_ref = refs[parts * chunks + 1]
    t = where_ref[0]
    n_p = out.shape[1]
    sub = rows * chunks
    for e in range(chunks):
        mine = ins[e * parts]
        n_r = mine.shape[0]
        bounds = [None] + [head_of(ins[e * parts + d]) for d in range(1, parts)]
        for l in range(n_p // LANES):
            total = mine[:, l * LANES : (l + 1) * LANES]
            for d in range(1, parts):
                at = HEAD + l * n_r
                total = total + decode(ins[e * parts + d][at : at + n_r, :], bounds[d])
            total = total.reshape(parts, 2, rows, LANES)
            for i in range(parts):
                at = pl.multiple_of((t ^ i) * sub + e * rows, 8)
                for part in range(2):
                    k_ref[
                        part, pl.ds(at, rows), l * LANES : (l + 1) * LANES
                    ] = total[i, part]
    for part in range(2):
        out[part] = k_ref[part].T


def stationary(n_row, n_col, pair_cc, screened, pair_vv):
    parts, cores, chunks = n_col, n_row // n_col, CHUNKS
    n_q, width = pair_vv.shape[1:]
    n_p, n_k = pair_cc.shape[1:]
    n_g = screened.shape[1]
    sub = n_q // parts
    rows = sub // chunks
    group = parts * 2 * rows
    r, z = lax.axis_index("row"), lax.axis_index("col")
    t, core = r // cores, r % cores
    where = jnp.stack([t, core, z, t ^ z]).astype(jnp.int32)

    def plane(x, i):
        pairs = [(a, ((a // cores) ^ i) * cores + a % cores) for a in range(n_row)]
        return lax.ppermute(x, "row", pairs)

    def twin(x, c):
        return lax.ppermute(x, "row", [(a, a ^ c) for a in range(n_row)])

    def along(x, d):
        return lax.ppermute(x, "col", [(a, a ^ d) for a in range(parts)])

    def route(arrays, name):
        outs = [jax.ShapeDtypeStruct(a.shape, a.dtype) for a in arrays]
        return call(
            functools.partial(route_body, parts), outs, [], name, [where, *arrays]
        )

    def twins(arrays):
        return list(arrays) + [twin(a, c) for c in range(1, cores) for a in arrays]

    with jax.named_scope("spread_vv"):
        cut = pair_vv.reshape(2, parts, sub, width)
        mine = [
            lax.dynamic_index_in_dim(cut, t ^ i, 1, keepdims=False).reshape(
                2 * sub, width
            )
            for i in range(parts)
        ]
        mine = [mine[0]] + [plane(mine[i], i) for i in range(1, parts)]
        mine = route(mine, "route_vv")
        mine = [mine[0]] + [along(mine[d], d) for d in range(1, parts)]
    finals = []
    for e in range(chunks):
        with jax.named_scope("gather_vv"):
            own = jnp.stack(
                [
                    m.reshape(2, sub, width)[:, e * rows : (e + 1) * rows]
                    for m in mine
                ]
            ).reshape(group, width)
            groups = twins([own] + [plane(own, i) for i in range(1, parts)])
        with jax.named_scope("inner"):
            coded = jax.ShapeDtypeStruct((HEAD + n_g // LANES * group, LANES), BF)
            inner = call(
                functools.partial(inner_body, parts, cores, rows),
                [coded] * parts,
                [
                    pltpu.VMEM((parts * group, cores * width), BF),
                    pltpu.VMEM((parts, n_g // LANES, group, LANES), F32),
                ],
                "inner",
                [where, screened, *groups],
                flops=2 * parts * group * cores * width * 2 * n_g,
            )
        with jax.named_scope("move_inner"):
            inner = [inner[0]] + [plane(inner[i], i) for i in range(1, parts)]
            inner = route(inner, "route_inner")
            inner = [inner[0]] + [along(inner[d], d) for d in range(1, parts)]
        with jax.named_scope("sum_inner"):
            (total,) = call(
                functools.partial(sum_body, parts),
                [coded],
                [pltpu.VMEM((n_g // LANES, group, LANES), F32)],
                "sum_inner",
                [where, *inner],
            )
        with jax.named_scope("gather_inner"):
            totals = twins([total] + [plane(total, i) for i in range(1, parts)])
        with jax.named_scope("outer"):
            term = jax.ShapeDtypeStruct((HEAD + n_p // LANES * group, LANES), BF)
            outer = call(
                functools.partial(outer_body, parts, cores, rows),
                [jax.ShapeDtypeStruct((group, n_p), F32)] + [term] * (parts - 1),
                [pltpu.VMEM((parts * group, n_k), BF)] * 2,
                "outer",
                [where, pair_cc, *totals],
                flops=4 * parts * group * n_k * 2 * n_p,
            )
        with jax.named_scope("move_outer"):
            finals += [outer[0]] + [along(outer[d], d) for d in range(1, parts)]
    with jax.named_scope("sum_outer"):
        (result,) = call(
            functools.partial(last_body, parts, chunks, rows),
            [jax.ShapeDtypeStruct((2, n_p, n_q), F32)],
            [pltpu.VMEM((2, n_q, n_p), F32)],
            "sum_outer",
            [where, *finals],
        )
    return result


def power_of_two(n):
    return n > 0 and n & (n - 1) == 0


def solution(mesh):
    placed = (P(None, "row", "col"), P(None, "row", "col"), P(None, "col", "row"))
    n_row, n_col = mesh.shape["row"], mesh.shape["col"]

    def shards(pair_cc, screened, pair_vv):
        n_q, width = pair_vv.shape[1:]
        n_p, n_k = pair_cc.shape[1:]
        n_g = screened.shape[1]
        fits = (
            power_of_two(n_row)
            and power_of_two(n_col)
            and n_row % n_col == 0
            and n_q % (n_col * CHUNKS * 16) == 0
            and width % LANES == 0
            and n_g == width
            and n_g % 256 == 0
            and n_p % LANES == 0
            and n_k == width * (n_row // n_col)
        )
        if not fits:
            return gathered(pair_cc, screened, pair_vv)
        return stationary(n_row, n_col, pair_cc, screened, pair_vv)

    return jax.shard_map(
        shards, mesh=mesh, in_specs=placed, out_specs=P(None, "row", "col"), check_vma=False
    )
```

```python
import functools

import jax
import jax.numpy as jnp
from jax import lax
from jax.experimental import pallas as pl
from jax.experimental.pallas import tpu as pltpu
from jax.sharding import PartitionSpec as P

LANES = 128
HEAD = 16
SPAN = 126.0
CHUNKS = 2
BF = jnp.bfloat16
F32 = jnp.float32


def half_nt(left, right):
    return lax.dot_general(
        left, right, (((1,), (1,)), ((), ())), preferred_element_type=jnp.float32
    )


def split_parts(values):
    upper = values.astype(jnp.bfloat16)
    lower = (values - upper.astype(jnp.float32)).astype(jnp.bfloat16)
    return (upper, lower)


def mixed_nn(data, inter):
    upper, lower = split_parts(inter)
    return jnp.dot(data, upper, preferred_element_type=jnp.float32) + jnp.dot(
        data, lower, preferred_element_type=jnp.float32
    )


def gathered(pair_cc, screened, pair_vv):
    cc_whole = lax.all_gather(pair_cc, "col", axis=2, tiled=True)
    vv_whole = lax.all_gather(pair_vv, "row", axis=2, tiled=True)
    piece = lax.all_gather(screened, "col", axis=2, tiled=True)
    inner_re = half_nt(piece[0], vv_whole[0]) - half_nt(piece[1], vv_whole[1])
    inner_im = half_nt(piece[0], vv_whole[1]) + half_nt(piece[1], vv_whole[0])
    right_block = jnp.stack([inner_re, inner_im])
    piece = lax.all_gather(right_block, "row", axis=1, tiled=True)
    out_re = mixed_nn(cc_whole[0], piece[0]) + mixed_nn(cc_whole[1], piece[1])
    out_im = mixed_nn(cc_whole[0], piece[1]) - mixed_nn(cc_whole[1], piece[0])
    return jnp.stack([out_re, out_im])


def bound_of(top):
    top = jnp.max(top, axis=(0, 1), keepdims=True)
    top = jnp.maximum(top, 1e-30) * (1.0 + 2.0**-7)
    return top.astype(BF).astype(F32)


def fold_top(values):
    return jnp.max(jnp.abs(values).reshape(-1, 8, LANES), axis=0)


def code(values, bound):
    return jnp.exp2(values * (SPAN / bound)).astype(BF)


def decode(coded, bound):
    return jnp.log2(coded.astype(F32)) * (bound * (1.0 / SPAN))


def head_of(ref):
    return ref[0:1, :].astype(F32)


def put_head(ref, bound):
    ref[0:HEAD, :] = jnp.broadcast_to(bound, (HEAD, LANES)).astype(BF)


def call(body, outs, scratch, name, args, flops=0):
    nbytes = sum(a.size * a.dtype.itemsize for a in args) + sum(
        functools.reduce(lambda p, q: p * q, o.shape) * o.dtype.itemsize for o in outs
    )
    specs = [pl.BlockSpec(memory_space=pltpu.SMEM)] + [
        pl.BlockSpec(memory_space=pltpu.VMEM)
    ] * (len(args) - 1)
    return pl.pallas_call(
        body,
        out_shape=outs,
        in_specs=specs,
        out_specs=[pl.BlockSpec(memory_space=pltpu.VMEM)] * len(outs),
        scratch_shapes=scratch,
        compiler_params=pltpu.CompilerParams(vmem_limit_bytes=24 * 1024 * 1024),
        cost_estimate=pl.CostEstimate(
            flops=flops, bytes_accessed=nbytes, transcendentals=0
        ),
        name=name,
    )(*args)


def spread_body(parts, chunks, where_ref, mine_ref, twin_ref, *outs):
    t, core = where_ref[0], where_ref[1]
    half, width = twin_ref.shape[1] // 2, twin_ref.shape[2]
    sub = half // parts
    rows = sub // chunks
    for i in range(parts):
        at = pl.multiple_of(core * half + (t ^ i) * sub, 16)
        for source in range(2):
            lane = pl.multiple_of((core ^ source) * width, LANES)
            ref = (mine_ref, twin_ref)[source]
            both = [ref[p, pl.ds(at, sub), :] for p in range(2)]
            both = [x.astype(F32).reshape(chunks, rows, width) for x in both]
            both = jnp.stack(both, axis=1).reshape(2 * sub, width)
            outs[i][:, pl.ds(lane, width)] = both.astype(BF)


def route_body(parts, where_ref, *refs):
    ins, outs = refs[:parts], refs[parts:]
    m = where_ref[2]
    for v in range(parts):

        @pl.when(m == v)
        def _(v=v):
            for d in range(parts):
                outs[d][...] = ins[v ^ d][...]


def chunk_body(parts, chunks, where_ref, *refs):
    ins, outs = refs[:parts], refs[parts:]
    step = outs[0].shape[0] // parts
    for e in range(chunks):
        for d in range(parts):
            outs[e][d * step : (d + 1) * step, :] = ins[d][e * step : (e + 1) * step, :]


def inner_body(parts, rows, where_ref, w_own_ref, w_twin_ref, *refs):
    ins, outs = refs[:parts], refs[parts : 2 * parts]
    x_ref, t_ref = refs[2 * parts :]
    group = ins[0].shape[0]
    for i in range(parts):
        x_ref[i * group : (i + 1) * group, :] = ins[i][...]
    n_g = w_own_ref.shape[1]
    tops = [jnp.zeros((8, LANES), F32) for _ in range(parts)]
    tile = 256
    for c, w_ref in enumerate((w_own_ref, w_twin_ref)):
        for g in range(0, n_g, tile):
            with_re = half_nt(x_ref[...], w_ref[0, g : g + tile, :])
            with_im = half_nt(x_ref[...], w_ref[1, g : g + tile, :])
            with_re = with_re.reshape(-1, 2, rows, tile)
            with_im = with_im.reshape(-1, 2, rows, tile)
            t_re = with_re[:, 0] - with_im[:, 1]
            t_im = with_im[:, 0] + with_re[:, 1]
            both = jnp.stack([t_re, t_im], axis=1).reshape(-1, tile)
            for i in range(parts):
                mine = both[i * group : (i + 1) * group]
                for l in range(0, tile, LANES):
                    block = mine[:, l : l + LANES]
                    tops[i] = jnp.maximum(tops[i], fold_top(block))
                    t_ref[i, (c * n_g + g + l) // LANES] = block
    for i in range(parts):
        bound = bound_of(tops[i])
        put_head(outs[i], bound)
        for l in range(2 * n_g // LANES):
            at = HEAD + l * group
            outs[i][at : at + group, :] = code(t_ref[i, l], bound)


def sum_body(parts, where_ref, *refs):
    ins, out = refs[:parts], refs[parts]
    t_ref = refs[parts + 1]
    n_l, group = t_ref.shape[0], t_ref.shape[1]
    step = group // parts
    top = jnp.zeros((8, LANES), F32)
    bounds = [head_of(ins[d]) for d in range(parts)]
    for l in range(n_l):
        for s in range(parts):
            total = None
            for d in range(parts):
                at = HEAD + l * group + (s ^ d) * step
                term = decode(ins[d][at : at + step, :], bounds[d])
                total = term if total is None else total + term
            top = jnp.maximum(top, fold_top(total))
            t_ref[l, s * step : (s + 1) * step, :] = total
    bound = bound_of(top)
    put_head(out, bound)
    for l in range(n_l):
        at = HEAD + l * group
        out[at : at + group, :] = code(t_ref[l], bound)


def outer_body(parts, rows, where_ref, a_own_ref, a_twin_ref, *refs):
    ins, outs = refs[:parts], refs[parts : 2 * parts]
    hi_ref, lo_ref = refs[2 * parts :]
    core = where_ref[1]
    n_l = hi_ref.shape[1] // LANES
    group = (ins[0].shape[0] - HEAD) // n_l
    for i in range(parts):
        bound = head_of(ins[i])
        for l in range(n_l):
            at = HEAD + l * group
            upper, lower = split_parts(decode(ins[i][at : at + group, :], bound))
            c, rest = divmod(l, n_l // 2)
            lane = pl.multiple_of(((core ^ c) * (n_l // 2) + rest) * LANES, LANES)
            hi_ref[i * group : (i + 1) * group, pl.ds(lane, LANES)] = upper
            lo_ref[i * group : (i + 1) * group, pl.ds(lane, LANES)] = lower
    n_p = a_own_ref.shape[1]
    tops = [jnp.zeros((8, LANES), F32) for _ in range(parts)]
    blocks = [[] for _ in range(parts)]
    for a_ref in (a_own_ref, a_twin_ref):
        with_re = half_nt(hi_ref[...], a_ref[0]) + half_nt(lo_ref[...], a_ref[0])
        with_im = half_nt(hi_ref[...], a_ref[1]) + half_nt(lo_ref[...], a_ref[1])
        with_re = with_re.reshape(parts, parts, 2, rows, n_p)
        with_im = with_im.reshape(parts, parts, 2, rows, n_p)
        k_re = with_re[:, :, 0] + with_im[:, :, 1]
        k_im = with_re[:, :, 1] - with_im[:, :, 0]
        for d in range(parts):
            both = jnp.stack([k_re[:, d], k_im[:, d]], axis=1).reshape(-1, n_p)
            for l in range(0, n_p, LANES):
                block = both[:, l : l + LANES]
                if d:
                    tops[d] = jnp.maximum(tops[d], fold_top(block))
                blocks[d].append(block)
    for d in range(parts):
        n_r = blocks[d][0].shape[0]
        if d == 0:
            for l, block in enumerate(blocks[0]):
                outs[0][l * n_r : (l + 1) * n_r, :] = block
            continue
        bound = bound_of(tops[d])
        put_head(outs[d], bound)
        for l, block in enumerate(blocks[d]):
            at = HEAD + l * n_r
            outs[d][at : at + n_r, :] = code(block, bound)


def last_body(parts, chunks, rows, where_ref, *refs):
    ins, outs = refs[: parts * chunks], refs[parts * chunks :]
    t = where_ref[0]
    sub = rows * chunks
    n_l = outs[0].shape[2] // LANES
    for e in range(chunks):
        mine = ins[e * parts]
        n_r = mine.shape[0] // (2 * n_l)
        bounds = [None] + [head_of(ins[e * parts + d]) for d in range(1, parts)]
        for l in range(2 * n_l):
            total = mine[l * n_r : (l + 1) * n_r, :]
            for d in range(1, parts):
                at = HEAD + l * n_r
                total = total + decode(ins[e * parts + d][at : at + n_r, :], bounds[d])
            total = total.reshape(parts, 2, rows, LANES)
            out, lane = outs[l // n_l], l % n_l * LANES
            for i in range(parts):
                at = pl.multiple_of((t ^ i) * sub + e * rows, 8)
                for part in range(2):
                    out[part, pl.ds(at, rows), lane : lane + LANES] = total[i, part]


def turn_body(where_ref, own_ref, twin_ref, out_ref, k_ref):
    core = where_ref[1]
    half = own_ref.shape[1]
    for c, ref in enumerate((own_ref, twin_ref)):
        at = pl.multiple_of((core ^ c) * half, 8)
        k_ref[:, pl.ds(at, half), :] = ref[...]
    for part in range(2):
        out_ref[part] = k_ref[part].T


def after(values, *earlier):
    return lax.optimization_barrier((tuple(values), earlier))[0]


def stationary(n_row, n_col, pair_cc, screened, pair_vv):
    parts, chunks = n_col, CHUNKS
    n_q, width = pair_vv.shape[1:]
    n_p, n_k = pair_cc.shape[1:]
    n_g = screened.shape[1]
    half = n_q // 2
    sub = half // parts
    rows = sub // chunks
    group = parts * 2 * rows
    r, z = lax.axis_index("row"), lax.axis_index("col")
    t, core = r // 2, r % 2
    where = jnp.stack([t, core, t ^ z]).astype(jnp.int32)
    shape = jax.ShapeDtypeStruct
    total_g = 2 * n_g

    def plane(x, i):
        pairs = [(a, a ^ (2 * i)) for a in range(n_row)]
        return lax.ppermute(x, "row", pairs)

    def twin(x):
        return lax.ppermute(x, "row", [(a, a ^ 1) for a in range(n_row)])

    def along(x, d):
        return lax.ppermute(x, "col", [(a, a ^ d) for a in range(parts)])

    def planes(arrays):
        return [arrays[0]] + [plane(arrays[i], i) for i in range(1, parts)]

    def alongs(arrays):
        return [arrays[0]] + [along(arrays[d], d) for d in range(1, parts)]

    def route(arrays, name):
        outs = [shape(a.shape, a.dtype) for a in arrays]
        return call(
            functools.partial(route_body, parts), outs, [], name, [where, *arrays]
        )

    with jax.named_scope("spread_vv"):
        theirs = twin(pair_vv)
        cut = call(
            functools.partial(spread_body, parts, chunks),
            [shape((2 * sub, 2 * width), BF)] * parts,
            [],
            "spread_vv",
            [where, pair_vv, theirs],
        )
        late = after([screened, pair_cc], *cut)
        screened_twin, pair_cc_twin = twin(late[0]), twin(late[1])
        cut = alongs(route(planes(cut), "route_vv"))
        cut = after(cut, screened_twin, pair_cc_twin)
        own = call(
            functools.partial(chunk_body, parts, chunks),
            [shape((group, 2 * width), BF)] * chunks,
            [],
            "chunk_vv",
            [where, *cut],
        )
    coded = shape((HEAD + total_g // LANES * group, LANES), BF)
    term = shape((HEAD + 2 * n_p // LANES * group, LANES), BF)

    def inner_of(groups):
        return call(
            functools.partial(inner_body, parts, rows),
            [coded] * parts,
            [
                pltpu.VMEM((parts * group, 2 * width), BF),
                pltpu.VMEM((parts, total_g // LANES, group, LANES), F32),
            ],
            "inner",
            [where, screened, screened_twin, *groups],
            flops=2 * parts * group * 2 * width * 2 * total_g,
        )

    def sum_of(arrays):
        (total,) = call(
            functools.partial(sum_body, parts),
            [coded],
            [pltpu.VMEM((total_g // LANES, group, LANES), F32)],
            "sum_inner",
            [where, *arrays],
        )
        return total

    def outer_of(arrays):
        return call(
            functools.partial(outer_body, parts, rows),
            [shape((2 * n_p // LANES * group, LANES), F32)] + [term] * (parts - 1),
            [pltpu.VMEM((parts * group, n_k), BF)] * 2,
            "outer",
            [where, pair_cc, pair_cc_twin, *arrays],
            flops=4 * parts * group * n_k * 4 * n_p,
        )

    with jax.named_scope("inner"):
        groups = [planes([own[e]] * parts) for e in range(chunks)]
        inner, routed = [], []
        for e in range(chunks):
            got = groups[e] if e == 0 else after(groups[e], *inner[e - 1])
            inner.append(inner_of(got))
    with jax.named_scope("move_inner"):
        for e in range(chunks):
            spread = planes(inner[e])
            if e + 1 < chunks:
                spread = after(spread, *inner[e + 1])
            routed.append(route(spread, "route_inner"))
        moved = [alongs(x) for x in routed]
    finals, outer = [], None
    with jax.named_scope("outer"):
        for e in range(chunks):
            got = moved[e] if e == 0 else after(moved[e], *outer)
            total = sum_of(got)
            outer = outer_of(planes([total] * parts))
            finals += alongs(outer)
    with jax.named_scope("sum_outer"):
        own, theirs = call(
            functools.partial(last_body, parts, chunks, rows),
            [shape((2, half, n_p), F32)] * 2,
            [],
            "sum_outer",
            [where, *finals],
        )
        (result,) = call(
            turn_body,
            [shape((2, n_p, n_q), F32)],
            [pltpu.VMEM((2, n_q, n_p), F32)],
            "turn",
            [where, own, twin(theirs)],
        )
    return result


def power_of_two(n):
    return n > 0 and n & (n - 1) == 0


def solution(mesh):
    placed = (P(None, "row", "col"), P(None, "row", "col"), P(None, "col", "row"))
    n_row, n_col = mesh.shape["row"], mesh.shape["col"]

    def shards(pair_cc, screened, pair_vv):
        n_q, width = pair_vv.shape[1:]
        n_p, n_k = pair_cc.shape[1:]
        n_g = screened.shape[1]
        fits = (
            power_of_two(n_row)
            and power_of_two(n_col)
            and n_row == 2 * n_col
            and n_q % (2 * n_col * CHUNKS * 8) == 0
            and n_q % (2 * n_col * 16) == 0
            and width % LANES == 0
            and n_g == width
            and n_g % 256 == 0
            and n_p % LANES == 0
            and n_k == 2 * width
        )
        if not fits:
            return gathered(pair_cc, screened, pair_vv)
        return stationary(n_row, n_col, pair_cc, screened, pair_vv)

    return jax.shard_map(
        shards, mesh=mesh, in_specs=placed, out_specs=P(None, "row", "col"), check_vma=False
    )
```

```python
import functools

import jax
import jax.numpy as jnp
from jax import lax
from jax.experimental import pallas as pl
from jax.experimental.pallas import tpu as pltpu
from jax.sharding import PartitionSpec as P

LANES = 128
HEAD = 16
SPAN = 126.0
CHUNKS = 2
MERGE = True
BATCHES = ((0, 1, 2), (3,))
ORDER = {"out_1": ["out_0"]}
FORWARD = {"p3_0": False, "p3_1": False, "q3_0": False, "q3_1": False}
HALVE = {"q2_0": True, "q2_1": True, "o_0": False, "o_1": True}
BF = jnp.bfloat16
F32 = jnp.float32


def half_nt(left, right):
    return lax.dot_general(
        left, right, (((1,), (1,)), ((), ())), preferred_element_type=jnp.float32
    )


def split_parts(values):
    upper = values.astype(jnp.bfloat16)
    lower = (values - upper.astype(jnp.float32)).astype(jnp.bfloat16)
    return (upper, lower)


def mixed_nn(data, inter):
    upper, lower = split_parts(inter)
    return jnp.dot(data, upper, preferred_element_type=jnp.float32) + jnp.dot(
        data, lower, preferred_element_type=jnp.float32
    )


def gathered(pair_cc, screened, pair_vv):
    cc_whole = lax.all_gather(pair_cc, "col", axis=2, tiled=True)
    vv_whole = lax.all_gather(pair_vv, "row", axis=2, tiled=True)
    piece = lax.all_gather(screened, "col", axis=2, tiled=True)
    inner_re = half_nt(piece[0], vv_whole[0]) - half_nt(piece[1], vv_whole[1])
    inner_im = half_nt(piece[0], vv_whole[1]) + half_nt(piece[1], vv_whole[0])
    right_block = jnp.stack([inner_re, inner_im])
    piece = lax.all_gather(right_block, "row", axis=1, tiled=True)
    out_re = mixed_nn(cc_whole[0], piece[0]) + mixed_nn(cc_whole[1], piece[1])
    out_im = mixed_nn(cc_whole[0], piece[1]) - mixed_nn(cc_whole[1], piece[0])
    return jnp.stack([out_re, out_im])


def bound_of(top):
    top = jnp.max(top, axis=(0, 1), keepdims=True)
    top = jnp.maximum(top, 1e-30) * (1.0 + 2.0**-7)
    return top.astype(BF).astype(F32)


def fold_top(values):
    return jnp.max(jnp.abs(values).reshape(-1, 8, LANES), axis=0)


def code(values, bound):
    return jnp.exp2(values * (SPAN / bound)).astype(BF)


def decode(coded, bound):
    return jnp.log2(coded.astype(F32)) * (bound * (1.0 / SPAN))


def head_of(ref):
    return ref[0:1, :].astype(F32)


def spread_head(bound):
    return jnp.broadcast_to(bound, (HEAD, LANES)).astype(BF)


def put_head(ref, bound):
    ref[0:HEAD, :] = spread_head(bound)


def call(body, outs, scratch, name, args, flops=0, far=0):
    specs = (
        [pl.BlockSpec(memory_space=pltpu.SMEM)]
        + [pl.BlockSpec(memory_space=pltpu.HBM)] * far
        + [pl.BlockSpec(memory_space=pltpu.VMEM)] * (len(args) - 1 - far)
    )
    return pl.pallas_call(
        body,
        out_shape=outs,
        in_specs=specs,
        out_specs=[pl.BlockSpec(memory_space=pltpu.VMEM)] * len(outs),
        scratch_shapes=scratch,
        compiler_params=pltpu.CompilerParams(vmem_limit_bytes=24 * 1024 * 1024),
        cost_estimate=pl.CostEstimate(
            flops=1, bytes_accessed=1, transcendentals=0
        ),
        name=name,
    )(*args)


def spread_body(parts, chunks, where_ref, mine_ref, twin_ref, *outs):
    t, core = where_ref[0], where_ref[1]
    half, width = twin_ref.shape[1] // 2, twin_ref.shape[2]
    sub = half // parts
    rows = sub // chunks
    for i in range(parts):
        at = pl.multiple_of(core * half + (t ^ i) * sub, 16)
        for source in range(2):
            lane = pl.multiple_of((core ^ source) * width, LANES)
            ref = (mine_ref, twin_ref)[source]
            both = [ref[p, pl.ds(at, sub), :] for p in range(2)]
            both = [x.astype(F32).reshape(chunks, rows, width) for x in both]
            both = jnp.stack(both, axis=1).reshape(2 * sub, width)
            outs[i][:, pl.ds(lane, width)] = both.astype(BF)


def route_body(parts, where_ref, *refs):
    ins, outs = refs[:parts], refs[parts:]
    m = where_ref[2]
    for v in range(parts):

        @pl.when(m == v)
        def _(v=v):
            for d in range(parts):
                outs[d][...] = ins[v ^ d][...]


def chunk_body(parts, chunks, where_ref, *refs):
    ins, outs = refs[:parts], refs[parts:]
    step = ins[0].shape[0] // chunks
    size = parts * step * chunks // len(outs)
    for e in range(chunks):
        for d in range(parts):
            at = (e * parts + d) * step
            out = outs[at // size]
            out[at % size : at % size + step, :] = ins[d][e * step : (e + 1) * step, :]


def fetch_body(where_ref, far_ref, near_ref, sem):
    copy = pltpu.make_async_copy(far_ref, near_ref, sem)
    copy.start()
    copy.wait()


def inner_body(n, chunks, rows, where_ref, w_own_ref, w_twin_ref, *refs):
    ins, outs = refs[:n], refs[n : n + n * chunks]
    x_ref, t_ref = refs[n + n * chunks :]
    size = ins[0].shape[0]
    group = size // chunks
    for i in range(n):
        x_ref[i * size : (i + 1) * size, :] = ins[i][...]
    n_g = w_own_ref.shape[1]
    tops = [jnp.zeros((8, LANES), F32) for _ in range(n * chunks)]
    tile = 256
    for c, w_ref in enumerate((w_own_ref, w_twin_ref)):
        for g in range(0, n_g, tile):
            with_re = half_nt(x_ref[...], w_ref[0, g : g + tile, :])
            with_im = half_nt(x_ref[...], w_ref[1, g : g + tile, :])
            with_re = with_re.reshape(-1, 2, rows, tile)
            with_im = with_im.reshape(-1, 2, rows, tile)
            t_re = with_re[:, 0] - with_im[:, 1]
            t_im = with_im[:, 0] + with_re[:, 1]
            both = jnp.stack([t_re, t_im], axis=1).reshape(-1, tile)
            for i in range(n * chunks):
                mine = both[i * group : (i + 1) * group]
                for l in range(0, tile, LANES):
                    block = mine[:, l : l + LANES]
                    tops[i] = jnp.maximum(tops[i], fold_top(block))
                    t_ref[i, (c * n_g + g + l) // LANES] = block
    for i in range(n * chunks):
        bound = bound_of(tops[i])
        put_head(outs[i], bound)
        for l in range(2 * n_g // LANES):
            at = HEAD + l * group
            outs[i][at : at + group, :] = code(t_ref[i, l], bound)


def deal_body(parts, where_ref, *refs):
    ins, (own_ref, far_ref, sent_ref) = refs[:parts], refs[parts:]
    size = own_ref.shape[0]
    m = where_ref[2]
    for v in range(parts):

        @pl.when(m == v)
        def _(v=v):
            own_ref[...] = ins[v][...]
            far_ref[...] = ins[v ^ 2][...]
            sent_ref[0:size, :] = ins[v ^ 1][...]
            sent_ref[size:, :] = ins[v ^ 3][...]


def fold_body(parts, where_ref, own_ref, far_ref, got_ref, kept_ref, sent_ref, t_ref):
    n_l, group, _ = kept_ref.shape
    step = group // parts
    size = own_ref.shape[0]
    own_bound, far_bound = head_of(own_ref), head_of(far_ref)
    near_bound = head_of(got_ref)
    next_bound = got_ref[size : size + 1, :].astype(F32)
    top = jnp.zeros((8, LANES), F32)
    for l in range(n_l):
        for s in range(parts):
            here = HEAD + l * group + s * step
            there = HEAD + l * group + (s ^ 1) * step
            to = slice(s * step, (s + 1) * step)
            kept_ref[l, to, :] = decode(
                own_ref[here : here + step, :], own_bound
            ) + decode(got_ref[there : there + step, :], near_bound)
            there += size
            total = decode(far_ref[here : here + step, :], far_bound) + decode(
                got_ref[there : there + step, :], next_bound
            )
            top = jnp.maximum(top, fold_top(total))
            t_ref[l, to, :] = total
    bound = bound_of(top)
    put_head(sent_ref, bound)
    for l in range(n_l):
        at = HEAD + l * group
        sent_ref[at : at + group, :] = code(t_ref[l], bound)


def sum_body(parts, where_ref, kept_ref, got_ref, out_ref, t_ref):
    n_l, group, _ = kept_ref.shape
    step = group // parts
    bound = head_of(got_ref)
    top = jnp.zeros((8, LANES), F32)
    for l in range(n_l):
        for s in range(parts):
            there = HEAD + l * group + (s ^ 2) * step
            to = slice(s * step, (s + 1) * step)
            total = kept_ref[l, to, :] + decode(got_ref[there : there + step, :], bound)
            top = jnp.maximum(top, fold_top(total))
            t_ref[l, to, :] = total
    bound = bound_of(top)
    put_head(out_ref, bound)
    for l in range(n_l):
        at = HEAD + l * group
        out_ref[at : at + group, :] = code(t_ref[l], bound)


def add_body(parts, where_ref, *refs):
    ins, out, t_ref = refs[:parts], refs[parts], refs[parts + 1]
    n_l, group = t_ref.shape[0], t_ref.shape[1]
    step = group // parts
    top = jnp.zeros((8, LANES), F32)
    bounds = [head_of(ins[d]) for d in range(parts)]
    for l in range(n_l):
        for s in range(parts):
            total = None
            for d in range(parts):
                at = HEAD + l * group + (s ^ d) * step
                term = decode(ins[d][at : at + step, :], bounds[d])
                total = term if total is None else total + term
            top = jnp.maximum(top, fold_top(total))
            t_ref[l, s * step : (s + 1) * step, :] = total
    bound = bound_of(top)
    put_head(out, bound)
    for l in range(n_l):
        at = HEAD + l * group
        out[at : at + group, :] = code(t_ref[l], bound)


def outer_body(parts, rows, plain, n_out, where_ref, a_own_ref, a_twin_ref, *refs):
    ins, outs = refs[:parts], refs[parts : parts + n_out]
    hi_ref, lo_ref = refs[parts + n_out :]
    core = where_ref[1]
    n_l = hi_ref.shape[1] // LANES
    group = (ins[0].shape[0] - HEAD) // n_l
    for i in range(parts):
        bound = head_of(ins[i])
        for l in range(n_l):
            at = HEAD + l * group
            upper, lower = split_parts(decode(ins[i][at : at + group, :], bound))
            c, rest = divmod(l, n_l // 2)
            lane = pl.multiple_of(((core ^ c) * (n_l // 2) + rest) * LANES, LANES)
            hi_ref[i * group : (i + 1) * group, pl.ds(lane, LANES)] = upper
            lo_ref[i * group : (i + 1) * group, pl.ds(lane, LANES)] = lower
    n_p = a_own_ref.shape[1]
    tops = [jnp.zeros((8, LANES), F32) for _ in range(parts)]
    blocks = [[] for _ in range(parts)]
    for a_ref in (a_own_ref, a_twin_ref):
        with_re = half_nt(hi_ref[...], a_ref[0]) + half_nt(lo_ref[...], a_ref[0])
        with_im = half_nt(hi_ref[...], a_ref[1]) + half_nt(lo_ref[...], a_ref[1])
        with_re = with_re.reshape(parts, parts, 2, rows, n_p)
        with_im = with_im.reshape(parts, parts, 2, rows, n_p)
        k_re = with_re[:, :, 0] + with_im[:, :, 1]
        k_im = with_re[:, :, 1] - with_im[:, :, 0]
        for d in range(parts):
            both = jnp.stack([k_re[:, d], k_im[:, d]], axis=1).reshape(-1, n_p)
            for l in range(0, n_p, LANES):
                block = both[:, l : l + LANES]
                if d >= plain:
                    tops[d] = jnp.maximum(tops[d], fold_top(block))
                blocks[d].append(block)
    for d in range(parts):
        n_r = blocks[d][0].shape[0]
        if d < plain:
            for l, block in enumerate(blocks[d]):
                outs[d][l * n_r : (l + 1) * n_r, :] = block
            continue
        bound = bound_of(tops[d])
        out = outs[min(d, len(outs) - 1)]
        start = (d - min(d, len(outs) - 1)) * (HEAD + len(blocks[d]) * n_r)
        out[start : start + HEAD, :] = spread_head(bound)
        for l, block in enumerate(blocks[d]):
            at = start + HEAD + l * n_r
            out[at : at + n_r, :] = code(block, bound)


def halve_body(where_ref, own_ref, near_ref, got_ref, kept_ref, sent_ref):
    n_r = own_ref.shape[0]
    kept_ref[...] = own_ref[...] + decode(got_ref[HEAD : HEAD + n_r, :], head_of(got_ref))
    start = HEAD + n_r
    bound = got_ref[start : start + 1, :].astype(F32)
    near = near_ref[...] + decode(got_ref[start + HEAD :, :], bound)
    bound = bound_of(fold_top(near))
    sent_ref[0:HEAD, :] = spread_head(bound)
    sent_ref[HEAD:, :] = code(near, bound)


def last_body(parts, counts, rows, where_ref, *refs):
    ins, outs = list(refs[: sum(counts)]), refs[sum(counts) :]
    t = where_ref[0]
    sub = rows * len(counts)
    n_l = outs[0].shape[2] // LANES
    for e, count in enumerate(counts):
        mine, *others = [ins.pop(0) for _ in range(count)]
        n_r = mine.shape[0] // (2 * n_l)
        bounds = [head_of(x) for x in others]
        for l in range(2 * n_l):
            total = mine[l * n_r : (l + 1) * n_r, :]
            at = HEAD + l * n_r
            for x, bound in zip(others, bounds):
                total = total + decode(x[at : at + n_r, :], bound)
            total = total.reshape(parts, 2, rows, LANES)
            out, lane = outs[l // n_l], l % n_l * LANES
            for i in range(parts):
                at = pl.multiple_of((t ^ i) * sub + e * rows, 8)
                for part in range(2):
                    out[part, pl.ds(at, rows), lane : lane + LANES] = total[i, part]


def turn_body(where_ref, own_ref, twin_ref, out_ref, k_ref):
    core = where_ref[1]
    half = own_ref.shape[1]
    for c, ref in enumerate((own_ref, twin_ref)):
        at = pl.multiple_of((core ^ c) * half, 8)
        k_ref[:, pl.ds(at, half), :] = ref[...]
    for part in range(2):
        out_ref[part] = k_ref[part].T


def after(values, *earlier):
    return lax.optimization_barrier((tuple(values), earlier))[0]


def stationary(n_row, n_col, pair_cc, screened, pair_vv):
    parts, chunks = n_col, CHUNKS
    n_q, width = pair_vv.shape[1:]
    n_p, n_k = pair_cc.shape[1:]
    n_g = screened.shape[1]
    half = n_q // 2
    sub = half // parts
    rows = sub // chunks
    group = parts * 2 * rows
    r, z = lax.axis_index("row"), lax.axis_index("col")
    t, core = r // 2, r % 2
    where = jnp.stack([t, core, t ^ z]).astype(jnp.int32)
    shape = jax.ShapeDtypeStruct
    total_g = 2 * n_g

    def plane(x, i):
        pairs = [(a, a ^ (2 * i)) for a in range(n_row)]
        return lax.ppermute(x, "row", pairs)

    def twin(x):
        return lax.ppermute(x, "row", [(a, a ^ 1) for a in range(n_row)])

    def along(x, d):
        return lax.ppermute(x, "col", [(a, a ^ d) for a in range(parts)])

    def planes(arrays):
        return [arrays[0]] + [plane(arrays[i], i) for i in range(1, parts)]

    def alongs(arrays):
        return [arrays[0]] + [along(arrays[d], d) for d in range(1, parts)]

    def route(arrays, name):
        outs = [shape(a.shape, a.dtype) for a in arrays]
        return call(
            functools.partial(route_body, parts), outs, [], name, [where, *arrays]
        )

    def fetch(x):
        outs, scratch = [shape(x.shape, x.dtype)], [pltpu.SemaphoreType.DMA]
        return call(fetch_body, outs, scratch, "fetch", [where, x], far=1)[0]

    with jax.named_scope("spread_vv"):
        theirs = twin(pair_vv)
        mine = fetch(pair_vv)
        cut = call(
            functools.partial(spread_body, parts, chunks),
            [shape((2 * sub, 2 * width), BF)] * parts,
            [],
            "spread_vv",
            [where, mine, theirs],
        )
        late = after([screened, pair_cc], *cut)
        screened_twin, pair_cc_twin = twin(late[0]), twin(late[1])
        cut = alongs(route(planes(cut), "route_vv"))
        screened_own = fetch(late[0])
        cut = after(cut, screened_own, screened_twin, pair_cc_twin)
        own = call(
            functools.partial(chunk_body, parts, chunks),
            [shape((group * chunks, 2 * width), BF)]
            if MERGE
            else [shape((group, 2 * width), BF)] * chunks,
            [],
            "chunk_vv",
            [where, *cut],
        )
    coded = shape((HEAD + total_g // LANES * group, LANES), BF)
    term = shape((HEAD + 2 * n_p // LANES * group, LANES), BF)

    def inner_of(groups):
        n = len(groups)
        return call(
            functools.partial(inner_body, n, chunks, rows),
            [coded] * (n * chunks),
            [
                pltpu.VMEM((n * chunks * group, 2 * width), BF),
                pltpu.VMEM((n * chunks, total_g // LANES, group, LANES), F32),
            ],
            "inner",
            [where, screened_own, screened_twin, *groups],
        )

    summed = pltpu.VMEM((total_g // LANES, group, LANES), F32)

    def deal(arrays):
        outs = [coded, coded, shape((2 * coded.shape[0], LANES), BF)]
        body = functools.partial(deal_body, parts)
        return call(body, outs, [], "deal_inner", [where, *arrays])

    def fold(own, far, got):
        outs = [shape((total_g // LANES, group, LANES), F32), coded]
        body = functools.partial(fold_body, parts)
        return call(body, outs, [summed], "fold_inner", [where, own, far, got])

    def sum_of(kept, got):
        body = functools.partial(sum_body, parts)
        return call(body, [coded], [summed], "sum_inner", [where, kept, got])[0]

    def outer_of(arrays, halving):
        n_r = 2 * n_p // LANES * group
        whole = shape((n_r, LANES), F32)
        if halving:
            outs = [whole, whole, shape((2 * (HEAD + n_r), LANES), BF)]
        else:
            outs = [whole] + [term] * (parts - 1)
        plain = 2 if halving else 1
        return call(
            functools.partial(outer_body, parts, rows, plain, len(outs)),
            outs,
            [pltpu.VMEM((parts * group, n_k), BF)] * 2,
            "outer",
            [where, pair_cc, pair_cc_twin, *arrays],
        )

    done = {}

    def step(name, arrays):
        late = [a for other in ORDER.get(name, ()) for a in done[other]]
        return after(arrays, *late) if late else tuple(arrays)

    def tell(name, arrays):
        done[name] = list(arrays)
        return arrays

    def gathered_of(x, forward):
        if not forward:
            return planes([x] * parts)
        near = plane(x, 1)
        return [x, near, plane(x, 2), plane(near, 2)]

    def add(arrays):
        body = functools.partial(add_body, parts)
        return call(body, [coded], [summed], "add_inner", [where, *arrays])[0]

    def gather_vv(e):
        if MERGE and e:
            return tell(f"p3_{e}", done["p3_0"])
        (x,) = step(f"p3_{e}", [own[e]])
        return tell(f"p3_{e}", gathered_of(x, FORWARD[f"p3_{e}"]))

    def inner_step(e, groups):
        if e == 0:
            found = []
            for batch in BATCHES:
                found += inner_of([groups[i] for i in batch])
            tell("inner", found)
        return done["inner"][e::chunks]

    def spread_step(e, arrays):
        mine, *sent = step(f"q1_{e}", arrays)
        return tell(f"q1_{e}", planes([mine, *sent]))

    def deal_step(e, arrays):
        arrays = step(f"deal_{e}", arrays)
        if HALVE[f"q2_{e}"]:
            return tell(f"deal_{e}", deal(arrays))
        return tell(f"deal_{e}", route(arrays, "route_inner"))

    def move_step(e, arrays):
        arrays = step(f"s1_{e}", arrays)
        if not HALVE[f"q2_{e}"]:
            got = tell(f"s1_{e}", alongs(arrays))
            return tell(f"sum_{e}", [add(step(f"sum_{e}", got))])[0]
        mine, far, sent = arrays
        (got,) = tell(f"s1_{e}", [along(sent, 1)])
        kept, sent = tell(f"fold_{e}", fold(*step(f"fold_{e}", [mine, far, got])))
        (sent,) = step(f"s2_{e}", [sent])
        (got,) = tell(f"s2_{e}", [along(sent, 2)])
        return tell(f"sum_{e}", [sum_of(*step(f"sum_{e}", [kept, got]))])[0]

    def gather_step(e, x):
        (x,) = step(f"q3_{e}", [x])
        return tell(f"q3_{e}", gathered_of(x, FORWARD[f"q3_{e}"]))

    def outer_step(e, arrays):
        return tell(f"out_{e}", outer_of(step(f"out_{e}", arrays), HALVE[f"o_{e}"]))

    def final_step(e, arrays):
        arrays = step(f"o_{e}", arrays)
        if not HALVE[f"o_{e}"]:
            return tell(f"o_{e}", alongs(arrays))
        kept, near, sent = arrays
        kept, sent = call(
            halve_body,
            [shape(kept.shape, F32), term],
            [],
            "halve",
            [where, *step(f"half_{e}", [kept, near, along(sent, 2)])],
        )
        done[f"half_{e}"] = [kept, sent]
        return tell(f"o_{e}", [kept, along(sent, 1)])

    state = [None] * chunks
    stages = (
        lambda e, x: gather_vv(e),
        inner_step,
        spread_step,
        deal_step,
        move_step,
        gather_step,
        outer_step,
        final_step,
    )
    names = ("p3", "in", "q1", "deal", "s1", "q3", "out", "o")
    pending = [0] * chunks
    while min(pending) < len(stages):
        moved = False
        for e in range(chunks):
            n = pending[e]
            if n == len(stages):
                continue
            needs = [f"{names[n]}_{e}"]
            if names[n] == "s1":
                needs += [f"fold_{e}", f"s2_{e}", f"sum_{e}"]
            if names[n] == "o":
                needs += [f"half_{e}"]
            wanted = [o for name in needs for o in ORDER.get(name, ())]
            if any(o not in done and not o.endswith(f"_{e}") for o in wanted):
                continue
            state[e] = stages[n](e, state[e])
            pending[e] += 1
            moved = True
        assert moved
    finals = [x for e in range(chunks) for x in state[e]]
    counts = tuple(len(x) for x in state)
    with jax.named_scope("sum_outer"):
        own, theirs = call(
            functools.partial(last_body, parts, counts, rows),
            [shape((2, half, n_p), F32)] * 2,
            [],
            "sum_outer",
            [where, *finals],
        )
        (result,) = call(
            turn_body,
            [shape((2, n_p, n_q), F32)],
            [pltpu.VMEM((2, n_q, n_p), F32)],
            "turn",
            [where, own, twin(theirs)],
        )
    return result


def power_of_two(n):
    return n > 0 and n & (n - 1) == 0


def solution(mesh):
    placed = (P(None, "row", "col"), P(None, "row", "col"), P(None, "col", "row"))
    n_row, n_col = mesh.shape["row"], mesh.shape["col"]

    def shards(pair_cc, screened, pair_vv):
        n_q, width = pair_vv.shape[1:]
        n_p, n_k = pair_cc.shape[1:]
        n_g = screened.shape[1]
        fits = (
            power_of_two(n_row)
            and power_of_two(n_col)
            and n_row == 2 * n_col
            and n_col == 4
            and n_q % (2 * n_col * CHUNKS * 8) == 0
            and n_q % (2 * n_col * 16) == 0
            and width % LANES == 0
            and n_g == width
            and n_g % 256 == 0
            and n_p % LANES == 0
            and n_k == 2 * width
        )
        if not fits:
            return gathered(pair_cc, screened, pair_vv)
        return stationary(n_row, n_col, pair_cc, screened, pair_vv)

    return jax.shard_map(
        shards, mesh=mesh, in_specs=placed, out_specs=P(None, "row", "col"), check_vma=False
    )
```

```python
import functools

import jax
import jax.numpy as jnp
from jax import lax
from jax.experimental import pallas as pl
from jax.experimental.pallas import tpu as pltpu
from jax.sharding import PartitionSpec as P

LANES = 128
HEAD = 16
SPAN = 126.0
CHUNKS = 2
MERGE = True
CHAIN = False
BATCHES = ((0, 1, 2), (3,))
ORDER = {}
FORWARD = {"p3_0": False, "p3_1": False, "q3_0": False, "q3_1": False}
HALVE = {"q2_0": True, "q2_1": True}
BF = jnp.bfloat16
F32 = jnp.float32


def half_nt(left, right):
    return lax.dot_general(
        left, right, (((1,), (1,)), ((), ())), preferred_element_type=jnp.float32
    )


def split_parts(values):
    upper = values.astype(jnp.bfloat16)
    lower = (values - upper.astype(jnp.float32)).astype(jnp.bfloat16)
    return (upper, lower)


def mixed_nn(data, inter):
    upper, lower = split_parts(inter)
    return jnp.dot(data, upper, preferred_element_type=jnp.float32) + jnp.dot(
        data, lower, preferred_element_type=jnp.float32
    )


def gathered(pair_cc, screened, pair_vv):
    cc_whole = lax.all_gather(pair_cc, "col", axis=2, tiled=True)
    vv_whole = lax.all_gather(pair_vv, "row", axis=2, tiled=True)
    piece = lax.all_gather(screened, "col", axis=2, tiled=True)
    inner_re = half_nt(piece[0], vv_whole[0]) - half_nt(piece[1], vv_whole[1])
    inner_im = half_nt(piece[0], vv_whole[1]) + half_nt(piece[1], vv_whole[0])
    right_block = jnp.stack([inner_re, inner_im])
    piece = lax.all_gather(right_block, "row", axis=1, tiled=True)
    out_re = mixed_nn(cc_whole[0], piece[0]) + mixed_nn(cc_whole[1], piece[1])
    out_im = mixed_nn(cc_whole[0], piece[1]) - mixed_nn(cc_whole[1], piece[0])
    return jnp.stack([out_re, out_im])


def bound_of(top):
    top = jnp.max(top, axis=(0, 1), keepdims=True)
    top = jnp.maximum(top, 1e-30) * (1.0 + 2.0**-7)
    return top.astype(BF).astype(F32)


def fold_top(values):
    return jnp.max(jnp.abs(values).reshape(-1, 8, LANES), axis=0)


def code(values, bound):
    return jnp.exp2(values * (SPAN / bound)).astype(BF)


def decode(coded, bound):
    return jnp.log2(coded.astype(F32)) * (bound * (1.0 / SPAN))


def head_of(ref):
    return ref[0:1, :].astype(F32)


def spread_head(bound):
    return jnp.broadcast_to(bound, (HEAD, LANES)).astype(BF)


def put_head(ref, bound):
    ref[0:HEAD, :] = spread_head(bound)


COSTS = {"inner": 4.0, "outer": 3.0, "sum_inner": 0.8, "fold_inner": 0.9, "deal_inner": 0.7, "fetch": 0.9, "turn": 1.4}
SCALE = None


def guess(name):
    if SCALE is None:
        return None
    flops = int(COSTS.get(name, 0.6) * SCALE * 1.1e9)
    return pl.CostEstimate(flops=flops, bytes_accessed=0, transcendentals=0)


def call(body, outs, scratch, name, args, flops=0, far=0):
    specs = (
        [pl.BlockSpec(memory_space=pltpu.SMEM)]
        + [pl.BlockSpec(memory_space=pltpu.HBM)] * far
        + [pl.BlockSpec(memory_space=pltpu.VMEM)] * (len(args) - 1 - far)
    )
    return pl.pallas_call(
        body,
        out_shape=outs,
        in_specs=specs,
        out_specs=[pl.BlockSpec(memory_space=pltpu.VMEM)] * len(outs),
        scratch_shapes=scratch,
        compiler_params=pltpu.CompilerParams(vmem_limit_bytes=24 * 1024 * 1024),
        cost_estimate=guess(name),
        name=name,
    )(*args)


def spread_body(parts, chunks, where_ref, mine_ref, twin_ref, *outs):
    t, core = where_ref[0], where_ref[1]
    half, width = twin_ref.shape[1] // 2, twin_ref.shape[2]
    sub = half // parts
    rows = sub // chunks
    for i in range(parts):
        at = pl.multiple_of(core * half + (t ^ i) * sub, 16)
        for source in range(2):
            lane = pl.multiple_of((core ^ source) * width, LANES)
            ref = (mine_ref, twin_ref)[source]
            both = [ref[p, pl.ds(at, sub), :] for p in range(2)]
            both = [x.astype(F32).reshape(chunks, rows, width) for x in both]
            both = jnp.stack(both, axis=1).reshape(2 * sub, width)
            outs[i][:, pl.ds(lane, width)] = both.astype(BF)


def route_body(parts, where_ref, *refs):
    ins, outs = refs[:parts], refs[parts:]
    m = where_ref[2]
    for v in range(parts):

        @pl.when(m == v)
        def _(v=v):
            for d in range(parts):
                outs[d][...] = ins[v ^ d][...]


def chunk_body(parts, chunks, where_ref, *refs):
    ins, outs = refs[:parts], refs[parts:]
    step = ins[0].shape[0] // chunks
    size = parts * step * chunks // len(outs)
    for e in range(chunks):
        for d in range(parts):
            at = (e * parts + d) * step
            out = outs[at // size]
            out[at % size : at % size + step, :] = ins[d][e * step : (e + 1) * step, :]


def fetch_body(where_ref, far_ref, near_ref, sem):
    copy = pltpu.make_async_copy(far_ref, near_ref, sem)
    copy.start()
    copy.wait()


def inner_body(n, chunks, rows, where_ref, w_own_ref, w_twin_ref, *refs):
    ins, outs = refs[:n], refs[n : n + n * chunks]
    x_ref, t_ref = refs[n + n * chunks :]
    size = ins[0].shape[0]
    group = size // chunks
    for i in range(n):
        x_ref[i * size : (i + 1) * size, :] = ins[i][...]
    n_g = w_own_ref.shape[1]
    tops = [jnp.zeros((8, LANES), F32) for _ in range(n * chunks)]
    tile = 256
    for c, w_ref in enumerate((w_own_ref, w_twin_ref)):
        for g in range(0, n_g, tile):
            with_re = half_nt(x_ref[...], w_ref[0, g : g + tile, :])
            with_im = half_nt(x_ref[...], w_ref[1, g : g + tile, :])
            with_re = with_re.reshape(-1, 2, rows, tile)
            with_im = with_im.reshape(-1, 2, rows, tile)
            t_re = with_re[:, 0] - with_im[:, 1]
            t_im = with_im[:, 0] + with_re[:, 1]
            both = jnp.stack([t_re, t_im], axis=1).reshape(-1, tile)
            for i in range(n * chunks):
                mine = both[i * group : (i + 1) * group]
                for l in range(0, tile, LANES):
                    block = mine[:, l : l + LANES]
                    tops[i] = jnp.maximum(tops[i], fold_top(block))
                    t_ref[i, (c * n_g + g + l) // LANES] = block
    for i in range(n * chunks):
        bound = bound_of(tops[i])
        put_head(outs[i], bound)
        for l in range(2 * n_g // LANES):
            at = HEAD + l * group
            outs[i][at : at + group, :] = code(t_ref[i, l], bound)


def deal_body(parts, where_ref, *refs):
    ins, (own_ref, far_ref, sent_ref) = refs[:parts], refs[parts:]
    size = own_ref.shape[0]
    m = where_ref[2]
    for v in range(parts):

        @pl.when(m == v)
        def _(v=v):
            own_ref[...] = ins[v][...]
            far_ref[...] = ins[v ^ 2][...]
            sent_ref[0:size, :] = ins[v ^ 1][...]
            sent_ref[size:, :] = ins[v ^ 3][...]


def fold_body(parts, where_ref, own_ref, far_ref, got_ref, kept_ref, sent_ref, t_ref):
    n_l, group, _ = kept_ref.shape
    step = group // parts
    size = own_ref.shape[0]
    own_bound, far_bound = head_of(own_ref), head_of(far_ref)
    near_bound = head_of(got_ref)
    next_bound = got_ref[size : size + 1, :].astype(F32)
    top = jnp.zeros((8, LANES), F32)
    for l in range(n_l):
        for s in range(parts):
            here = HEAD + l * group + s * step
            there = HEAD + l * group + (s ^ 1) * step
            to = slice(s * step, (s + 1) * step)
            kept_ref[l, to, :] = decode(
                own_ref[here : here + step, :], own_bound
            ) + decode(got_ref[there : there + step, :], near_bound)
            there += size
            total = decode(far_ref[here : here + step, :], far_bound) + decode(
                got_ref[there : there + step, :], next_bound
            )
            top = jnp.maximum(top, fold_top(total))
            t_ref[l, to, :] = total
    bound = bound_of(top)
    put_head(sent_ref, bound)
    for l in range(n_l):
        at = HEAD + l * group
        sent_ref[at : at + group, :] = code(t_ref[l], bound)


def sum_body(parts, where_ref, kept_ref, got_ref, out_ref, t_ref):
    n_l, group, _ = kept_ref.shape
    step = group // parts
    bound = head_of(got_ref)
    top = jnp.zeros((8, LANES), F32)
    for l in range(n_l):
        for s in range(parts):
            there = HEAD + l * group + (s ^ 2) * step
            to = slice(s * step, (s + 1) * step)
            total = kept_ref[l, to, :] + decode(got_ref[there : there + step, :], bound)
            top = jnp.maximum(top, fold_top(total))
            t_ref[l, to, :] = total
    bound = bound_of(top)
    put_head(out_ref, bound)
    for l in range(n_l):
        at = HEAD + l * group
        out_ref[at : at + group, :] = code(t_ref[l], bound)


def add_body(parts, where_ref, *refs):
    ins, out, t_ref = refs[:parts], refs[parts], refs[parts + 1]
    n_l, group = t_ref.shape[0], t_ref.shape[1]
    step = group // parts
    top = jnp.zeros((8, LANES), F32)
    bounds = [head_of(ins[d]) for d in range(parts)]
    for l in range(n_l):
        for s in range(parts):
            total = None
            for d in range(parts):
                at = HEAD + l * group + (s ^ d) * step
                term = decode(ins[d][at : at + step, :], bounds[d])
                total = term if total is None else total + term
            top = jnp.maximum(top, fold_top(total))
            t_ref[l, s * step : (s + 1) * step, :] = total
    bound = bound_of(top)
    put_head(out, bound)
    for l in range(n_l):
        at = HEAD + l * group
        out[at : at + group, :] = code(t_ref[l], bound)


def outer_body(parts, rows, n_early, where_ref, a_own_ref, a_twin_ref, *refs):
    ins, early = refs[:parts], refs[parts : parts + n_early]
    outs, t_ref = refs[parts + n_early : -1], refs[-1]
    core = where_ref[1]
    n_l = t_ref.shape[1] // LANES
    group = (ins[0].shape[0] - HEAD) // n_l
    for i in range(parts):
        bound = head_of(ins[i])
        for l in range(n_l):
            at = HEAD + l * group
            upper, lower = split_parts(decode(ins[i][at : at + group, :], bound))
            c, rest = divmod(l, n_l // 2)
            lane = pl.multiple_of(((core ^ c) * (n_l // 2) + rest) * LANES, LANES)
            for at, half in ((i, upper), (parts + i, lower)):
                t_ref[at * group : (at + 1) * group, pl.ds(lane, LANES)] = half
    n_p = a_own_ref.shape[1]
    tops = [jnp.zeros((8, LANES), F32) for _ in range(parts)]
    blocks = [[] for _ in range(parts)]
    for a_ref in (a_own_ref, a_twin_ref):
        with_re = half_nt(t_ref[...], a_ref[0])
        with_im = half_nt(t_ref[...], a_ref[1])
        n_t = parts * group
        with_re = with_re[:n_t] + with_re[n_t:]
        with_im = with_im[:n_t] + with_im[n_t:]
        with_re = with_re.reshape(parts, parts, 2, rows, n_p)
        with_im = with_im.reshape(parts, parts, 2, rows, n_p)
        k_re = with_re[:, :, 0] + with_im[:, :, 1]
        k_im = with_re[:, :, 1] - with_im[:, :, 0]
        for d in range(parts):
            both = jnp.stack([k_re[:, d], k_im[:, d]], axis=1).reshape(-1, n_p)
            for l in range(0, n_p, LANES):
                block = both[:, l : l + LANES]
                if d:
                    tops[d] = jnp.maximum(tops[d], fold_top(block))
                blocks[d].append(block)
    for d in range(parts):
        n_r = blocks[d][0].shape[0]
        if d == 0:
            for l, block in enumerate(blocks[d]):
                outs[d][l * n_r : (l + 1) * n_r, :] = block
            continue
        bound = bound_of(tops[d])
        out, start = outs[d], 0
        if early:
            start = early[d - 1].shape[0]
            out[:start, :] = early[d - 1][...]
        out[start : start + HEAD, :] = spread_head(bound)
        for l, block in enumerate(blocks[d]):
            at = start + HEAD + l * n_r
            out[at : at + n_r, :] = code(block, bound)


def last_body(parts, chunks, rows, where_ref, *refs):
    own, others = refs[:chunks], refs[chunks : chunks + parts - 1]
    outs = refs[chunks + parts - 1 :]
    t = where_ref[0]
    sub = rows * chunks
    n_l = outs[0].shape[2] // LANES
    size = others[0].shape[0] // chunks
    for e in range(chunks):
        n_r = own[e].shape[0] // (2 * n_l)
        start = e * size
        bounds = [x[start : start + 1, :].astype(F32) for x in others]
        for l in range(2 * n_l):
            total = own[e][l * n_r : (l + 1) * n_r, :]
            at = start + HEAD + l * n_r
            for x, bound in zip(others, bounds):
                total = total + decode(x[at : at + n_r, :], bound)
            total = total.reshape(parts, 2, rows, LANES)
            out, lane = outs[l // n_l], l % n_l * LANES
            for i in range(parts):
                at = pl.multiple_of((t ^ i) * sub + e * rows, 8)
                for part in range(2):
                    out[part, pl.ds(at, rows), lane : lane + LANES] = total[i, part]


def turn_body(where_ref, own_ref, twin_ref, out_ref, k_ref):
    core = where_ref[1]
    half = own_ref.shape[1]
    for c, ref in enumerate((own_ref, twin_ref)):
        at = pl.multiple_of((core ^ c) * half, 8)
        k_ref[:, pl.ds(at, half), :] = ref[...]
    for part in range(2):
        out_ref[part] = k_ref[part].T


def after(values, *earlier):
    return lax.optimization_barrier((tuple(values), earlier))[0]


def stationary(n_row, n_col, pair_cc, screened, pair_vv):
    parts, chunks = n_col, CHUNKS
    n_q, width = pair_vv.shape[1:]
    n_p, n_k = pair_cc.shape[1:]
    n_g = screened.shape[1]
    half = n_q // 2
    sub = half // parts
    rows = sub // chunks
    group = parts * 2 * rows
    r, z = lax.axis_index("row"), lax.axis_index("col")
    t, core = r // 2, r % 2
    where = jnp.stack([t, core, t ^ z]).astype(jnp.int32)
    shape = jax.ShapeDtypeStruct
    total_g = 2 * n_g

    def plane(x, i):
        pairs = [(a, a ^ (2 * i)) for a in range(n_row)]
        return lax.ppermute(x, "row", pairs)

    def twin(x):
        return lax.ppermute(x, "row", [(a, a ^ 1) for a in range(n_row)])

    def along(x, d):
        return lax.ppermute(x, "col", [(a, a ^ d) for a in range(parts)])

    def planes(arrays):
        return [arrays[0]] + [plane(arrays[i], i) for i in range(1, parts)]

    def alongs(arrays):
        return [arrays[0]] + [along(arrays[d], d) for d in range(1, parts)]

    def route(arrays, name):
        outs = [shape(a.shape, a.dtype) for a in arrays]
        return call(
            functools.partial(route_body, parts), outs, [], name, [where, *arrays]
        )

    def fetch(x):
        outs, scratch = [shape(x.shape, x.dtype)], [pltpu.SemaphoreType.DMA]
        return call(fetch_body, outs, scratch, "fetch", [where, x], far=1)[0]

    with jax.named_scope("spread_vv"):
        theirs = twin(pair_vv)
        mine = fetch(pair_vv)
        cut = call(
            functools.partial(spread_body, parts, chunks),
            [shape((2 * sub, 2 * width), BF)] * parts,
            [],
            "spread_vv",
            [where, mine, theirs],
        )
        late = after([screened, pair_cc], *cut)
        screened_twin, pair_cc_twin = twin(late[0]), twin(late[1])
        cut = alongs(route(planes(cut), "route_vv"))
        screened_own = fetch(late[0])
        cut = after(cut, screened_own, screened_twin, pair_cc_twin)
        own = call(
            functools.partial(chunk_body, parts, chunks),
            [shape((group * chunks, 2 * width), BF)]
            if MERGE
            else [shape((group, 2 * width), BF)] * chunks,
            [],
            "chunk_vv",
            [where, *cut],
        )
    coded = shape((HEAD + total_g // LANES * group, LANES), BF)
    term = shape((HEAD + 2 * n_p // LANES * group, LANES), BF)

    def inner_of(groups):
        n = len(groups)
        return call(
            functools.partial(inner_body, n, chunks, rows),
            [coded] * (n * chunks),
            [
                pltpu.VMEM((n * chunks * group, 2 * width), BF),
                pltpu.VMEM((n * chunks, total_g // LANES, group, LANES), F32),
            ],
            "inner",
            [where, screened_own, screened_twin, *groups],
        )

    summed = pltpu.VMEM((total_g // LANES, group, LANES), F32)

    def deal(arrays):
        outs = [coded, coded, shape((2 * coded.shape[0], LANES), BF)]
        body = functools.partial(deal_body, parts)
        return call(body, outs, [], "deal_inner", [where, *arrays])

    def fold(own, far, got):
        outs = [shape((total_g // LANES, group, LANES), F32), coded]
        body = functools.partial(fold_body, parts)
        return call(body, outs, [summed], "fold_inner", [where, own, far, got])

    def sum_of(kept, got):
        body = functools.partial(sum_body, parts)
        return call(body, [coded], [summed], "sum_inner", [where, kept, got])[0]

    def outer_of(arrays, early):
        n_r = 2 * n_p // LANES * group
        sent = shape(((HEAD + n_r) * (2 if early else 1), LANES), BF)
        return call(
            functools.partial(outer_body, parts, rows, len(early)),
            [shape((n_r, LANES), F32)] + [sent] * (parts - 1),
            [pltpu.VMEM((2 * parts * group, n_k), BF)],
            "outer",
            [where, pair_cc, pair_cc_twin, *arrays, *early],
        )

    done = {}

    def step(name, arrays):
        late = [a for other in ORDER.get(name, ()) for a in done[other]]
        return after(arrays, *late) if late else tuple(arrays)

    def tell(name, arrays):
        done[name] = list(arrays)
        return arrays

    def gathered_of(x, forward):
        if not forward:
            return planes([x] * parts)
        near = plane(x, 1)
        return [x, near, plane(x, 2), plane(near, 2)]

    def add(arrays):
        body = functools.partial(add_body, parts)
        return call(body, [coded], [summed], "add_inner", [where, *arrays])[0]

    def gather_vv(e):
        if MERGE and e:
            return tell(f"p3_{e}", done["p3_0"])
        (x,) = step(f"p3_{e}", [own[e]])
        return tell(f"p3_{e}", gathered_of(x, FORWARD[f"p3_{e}"]))

    def inner_step(e, groups):
        if e == 0:
            found = []
            for batch in BATCHES:
                picked = [groups[i] for i in batch]
                if found and CHAIN:
                    picked = after(picked, *found)
                found += inner_of(picked)
            tell("inner", found)
        return done["inner"][e::chunks]

    def spread_step(e, arrays):
        mine, *sent = step(f"q1_{e}", arrays)
        return tell(f"q1_{e}", planes([mine, *sent]))

    def deal_step(e, arrays):
        arrays = step(f"deal_{e}", arrays)
        if HALVE[f"q2_{e}"]:
            return tell(f"deal_{e}", deal(arrays))
        return tell(f"deal_{e}", route(arrays, "route_inner"))

    def move_step(e, arrays):
        arrays = step(f"s1_{e}", arrays)
        if not HALVE[f"q2_{e}"]:
            got = tell(f"s1_{e}", alongs(arrays))
            return tell(f"sum_{e}", [add(step(f"sum_{e}", got))])[0]
        mine, far, sent = arrays
        (got,) = tell(f"s1_{e}", [along(sent, 1)])
        kept, sent = tell(f"fold_{e}", fold(*step(f"fold_{e}", [mine, far, got])))
        (sent,) = step(f"s2_{e}", [sent])
        (got,) = tell(f"s2_{e}", [along(sent, 2)])
        return tell(f"sum_{e}", [sum_of(*step(f"sum_{e}", [kept, got]))])[0]

    def gather_step(e, x):
        (x,) = step(f"q3_{e}", [x])
        return tell(f"q3_{e}", gathered_of(x, FORWARD[f"q3_{e}"]))

    def outer_step(e, arrays):
        early = done["out_0"][1:] if e else []
        return tell(f"out_{e}", outer_of(step(f"out_{e}", arrays), early))

    state = [None] * chunks
    stages = (
        lambda e, x: gather_vv(e),
        inner_step,
        spread_step,
        deal_step,
        move_step,
        gather_step,
        outer_step,
    )
    names = ("p3", "in", "q1", "deal", "s1", "q3", "out")
    pending = [0] * chunks
    while min(pending) < len(stages):
        moved = False
        for e in range(chunks):
            n = pending[e]
            if n == len(stages):
                continue
            needs = [f"{names[n]}_{e}"]
            if names[n] == "s1":
                needs += [f"fold_{e}", f"s2_{e}", f"sum_{e}"]
            wanted = [o for name in needs for o in ORDER.get(name, ())]
            if any(o not in done and not o.endswith(f"_{e}") for o in wanted):
                continue
            state[e] = stages[n](e, state[e])
            pending[e] += 1
            moved = True
        assert moved
    finals = [x[0] for x in state] + alongs(state[-1])[1:]
    with jax.named_scope("sum_outer"):
        own, theirs = call(
            functools.partial(last_body, parts, chunks, rows),
            [shape((2, half, n_p), F32)] * 2,
            [],
            "sum_outer",
            [where, *finals],
        )
        (result,) = call(
            turn_body,
            [shape((2, n_p, n_q), F32)],
            [pltpu.VMEM((2, n_q, n_p), F32)],
            "turn",
            [where, own, twin(theirs)],
        )
    return result


def power_of_two(n):
    return n > 0 and n & (n - 1) == 0


def solution(mesh):
    placed = (P(None, "row", "col"), P(None, "row", "col"), P(None, "col", "row"))
    n_row, n_col = mesh.shape["row"], mesh.shape["col"]

    def shards(pair_cc, screened, pair_vv):
        n_q, width = pair_vv.shape[1:]
        n_p, n_k = pair_cc.shape[1:]
        n_g = screened.shape[1]
        fits = (
            power_of_two(n_row)
            and power_of_two(n_col)
            and n_row == 2 * n_col
            and n_col == 4
            and n_q % (2 * n_col * CHUNKS * 8) == 0
            and n_q % (2 * n_col * 16) == 0
            and width % LANES == 0
            and n_g == width
            and n_g % 256 == 0
            and n_p % LANES == 0
            and n_k == 2 * width
        )
        if not fits:
            return gathered(pair_cc, screened, pair_vv)
        return stationary(n_row, n_col, pair_cc, screened, pair_vv)

    return jax.shard_map(
        shards, mesh=mesh, in_specs=placed, out_specs=P(None, "row", "col"), check_vma=False
    )
```

```python
import functools

import jax
import jax.numpy as jnp
from jax import lax
from jax.experimental import pallas as pl
from jax.experimental.pallas import tpu as pltpu
from jax.sharding import PartitionSpec as P

LANES = 128
HEAD = 16
VMEM_LIMIT = 24 * 1024 * 1024
SPAN = 126.0
CHUNKS = 2
BATCHES = ((0, 1, 2), (3,))
BF = jnp.bfloat16
F32 = jnp.float32


def half_nt(left, right):
    return lax.dot_general(
        left, right, (((1,), (1,)), ((), ())), preferred_element_type=jnp.float32
    )


def split_parts(values):
    upper = values.astype(jnp.bfloat16)
    lower = (values - upper.astype(jnp.float32)).astype(jnp.bfloat16)
    return (upper, lower)


def mixed_nn(data, inter):
    upper, lower = split_parts(inter)
    return jnp.dot(data, upper, preferred_element_type=jnp.float32) + jnp.dot(
        data, lower, preferred_element_type=jnp.float32
    )


def gathered(pair_cc, screened, pair_vv):
    cc_whole = lax.all_gather(pair_cc, "col", axis=2, tiled=True)
    vv_whole = lax.all_gather(pair_vv, "row", axis=2, tiled=True)
    piece = lax.all_gather(screened, "col", axis=2, tiled=True)
    inner_re = half_nt(piece[0], vv_whole[0]) - half_nt(piece[1], vv_whole[1])
    inner_im = half_nt(piece[0], vv_whole[1]) + half_nt(piece[1], vv_whole[0])
    right_block = jnp.stack([inner_re, inner_im])
    piece = lax.all_gather(right_block, "row", axis=1, tiled=True)
    out_re = mixed_nn(cc_whole[0], piece[0]) + mixed_nn(cc_whole[1], piece[1])
    out_im = mixed_nn(cc_whole[0], piece[1]) - mixed_nn(cc_whole[1], piece[0])
    return jnp.stack([out_re, out_im])


def bound_of(top):
    top = jnp.max(top, axis=(0, 1), keepdims=True)
    top = jnp.maximum(top, 2e-36) * (1.0 + 2.0**-7)
    return top.astype(BF).astype(F32)


def fold_top(values):
    return jnp.max(jnp.abs(values).reshape(-1, 8, LANES), axis=0)


def code(values, bound):
    return jnp.exp2(values * (SPAN / bound)).astype(BF)


def decode(coded, bound):
    return jnp.log2(coded.astype(F32)) * (bound * (1.0 / SPAN))


def head_of(ref):
    return ref[0:1, :].astype(F32)


def spread_head(bound):
    return jnp.broadcast_to(bound, (HEAD, LANES)).astype(BF)


def put_head(ref, bound):
    ref[0:HEAD, :] = spread_head(bound)


def call(body, outs, scratch, name, args, far=0):
    specs = (
        [pl.BlockSpec(memory_space=pltpu.SMEM)]
        + [pl.BlockSpec(memory_space=pltpu.HBM)] * far
        + [pl.BlockSpec(memory_space=pltpu.VMEM)] * (len(args) - 1 - far)
    )
    return pl.pallas_call(
        body,
        out_shape=outs,
        in_specs=specs,
        out_specs=[pl.BlockSpec(memory_space=pltpu.VMEM)] * len(outs),
        scratch_shapes=scratch,
        compiler_params=pltpu.CompilerParams(vmem_limit_bytes=VMEM_LIMIT),
        name=name,
    )(*args)


def spread_body(parts, chunks, where_ref, mine_ref, twin_ref, *outs):
    t, core = where_ref[0], where_ref[1]
    half, width = twin_ref.shape[1] // 2, twin_ref.shape[2]
    sub = half // parts
    rows = sub // chunks
    for i in range(parts):
        at = pl.multiple_of(core * half + (t ^ i) * sub, 16)
        for source in range(2):
            lane = pl.multiple_of((core ^ source) * width, LANES)
            ref = (mine_ref, twin_ref)[source]
            both = [ref[p, pl.ds(at, sub), :] for p in range(2)]
            both = [x.astype(F32).reshape(chunks, rows, width) for x in both]
            both = jnp.stack(both, axis=1).reshape(2 * sub, width)
            outs[i][:, pl.ds(lane, width)] = both.astype(BF)


def route_body(parts, where_ref, *refs):
    ins, outs = refs[:parts], refs[parts:]
    m = where_ref[2]
    for v in range(parts):

        @pl.when(m == v)
        def _(v=v):
            for d in range(parts):
                outs[d][...] = ins[v ^ d][...]


def chunk_body(parts, chunks, where_ref, *refs):
    ins, outs = refs[:parts], refs[parts:]
    step = ins[0].shape[0] // chunks
    size = parts * step * chunks // len(outs)
    for e in range(chunks):
        for d in range(parts):
            at = (e * parts + d) * step
            out = outs[at // size]
            out[at % size : at % size + step, :] = ins[d][e * step : (e + 1) * step, :]


def fetch_body(where_ref, far_ref, near_ref, sem):
    copy = pltpu.make_async_copy(far_ref, near_ref, sem)
    copy.start()
    copy.wait()


def inner_body(n, chunks, rows, where_ref, w_own_ref, w_twin_ref, *refs):
    ins, outs = refs[:n], refs[n : n + n * chunks]
    x_ref, t_ref = refs[n + n * chunks :]
    size = ins[0].shape[0]
    group = size // chunks
    for i in range(n):
        x_ref[i * size : (i + 1) * size, :] = ins[i][...]
    n_g = w_own_ref.shape[1]
    tops = [jnp.zeros((8, LANES), F32) for _ in range(n * chunks)]
    tile = 256
    for c, w_ref in enumerate((w_own_ref, w_twin_ref)):
        for g in range(0, n_g, tile):
            with_re = half_nt(x_ref[...], w_ref[0, g : g + tile, :])
            with_im = half_nt(x_ref[...], w_ref[1, g : g + tile, :])
            with_re = with_re.reshape(-1, 2, rows, tile)
            with_im = with_im.reshape(-1, 2, rows, tile)
            t_re = with_re[:, 0] - with_im[:, 1]
            t_im = with_im[:, 0] + with_re[:, 1]
            both = jnp.stack([t_re, t_im], axis=1).reshape(-1, tile)
            for i in range(n * chunks):
                mine = both[i * group : (i + 1) * group]
                for l in range(0, tile, LANES):
                    block = mine[:, l : l + LANES]
                    tops[i] = jnp.maximum(tops[i], fold_top(block))
                    t_ref[i, (c * n_g + g + l) // LANES] = block
    for i in range(n * chunks):
        bound = bound_of(tops[i])
        put_head(outs[i], bound)
        for l in range(2 * n_g // LANES):
            at = HEAD + l * group
            outs[i][at : at + group, :] = code(t_ref[i, l], bound)


def deal_body(parts, where_ref, *refs):
    ins, (own_ref, far_ref, sent_ref) = refs[:parts], refs[parts:]
    size = own_ref.shape[0]
    m = where_ref[2]
    for v in range(parts):

        @pl.when(m == v)
        def _(v=v):
            own_ref[...] = ins[v][...]
            far_ref[...] = ins[v ^ 2][...]
            sent_ref[0:size, :] = ins[v ^ 1][...]
            sent_ref[size:, :] = ins[v ^ 3][...]


def fold_body(parts, where_ref, own_ref, far_ref, got_ref, kept_ref, sent_ref, t_ref):
    n_l, group, _ = kept_ref.shape
    step = group // parts
    size = own_ref.shape[0]
    own_bound, far_bound = head_of(own_ref), head_of(far_ref)
    near_bound = head_of(got_ref)
    next_bound = got_ref[size : size + 1, :].astype(F32)
    top = jnp.zeros((8, LANES), F32)
    for l in range(n_l):
        for s in range(parts):
            here = HEAD + l * group + s * step
            there = HEAD + l * group + (s ^ 1) * step
            to = slice(s * step, (s + 1) * step)
            kept_ref[l, to, :] = decode(
                own_ref[here : here + step, :], own_bound
            ) + decode(got_ref[there : there + step, :], near_bound)
            there += size
            total = decode(far_ref[here : here + step, :], far_bound) + decode(
                got_ref[there : there + step, :], next_bound
            )
            top = jnp.maximum(top, fold_top(total))
            t_ref[l, to, :] = total
    bound = bound_of(top)
    put_head(sent_ref, bound)
    for l in range(n_l):
        at = HEAD + l * group
        sent_ref[at : at + group, :] = code(t_ref[l], bound)


def sum_body(parts, where_ref, kept_ref, got_ref, out_ref, t_ref):
    n_l, group, _ = kept_ref.shape
    step = group // parts
    bound = head_of(got_ref)
    top = jnp.zeros((8, LANES), F32)
    for l in range(n_l):
        for s in range(parts):
            there = HEAD + l * group + (s ^ 2) * step
            to = slice(s * step, (s + 1) * step)
            total = kept_ref[l, to, :] + decode(got_ref[there : there + step, :], bound)
            top = jnp.maximum(top, fold_top(total))
            t_ref[l, to, :] = total
    bound = bound_of(top)
    put_head(out_ref, bound)
    for l in range(n_l):
        at = HEAD + l * group
        out_ref[at : at + group, :] = code(t_ref[l], bound)


def outer_body(parts, rows, n_early, where_ref, a_own_ref, a_twin_ref, *refs):
    ins, early = refs[:parts], refs[parts : parts + n_early]
    outs, t_ref = refs[parts + n_early : -1], refs[-1]
    core = where_ref[1]
    n_l = t_ref.shape[1] // LANES
    group = (ins[0].shape[0] - HEAD) // n_l
    for i in range(parts):
        bound = head_of(ins[i])
        for l in range(n_l):
            at = HEAD + l * group
            upper, lower = split_parts(decode(ins[i][at : at + group, :], bound))
            c, rest = divmod(l, n_l // 2)
            lane = pl.multiple_of(((core ^ c) * (n_l // 2) + rest) * LANES, LANES)
            for at, half in ((i, upper), (parts + i, lower)):
                t_ref[at * group : (at + 1) * group, pl.ds(lane, LANES)] = half
    n_p = a_own_ref.shape[1]
    tops = [jnp.zeros((8, LANES), F32) for _ in range(parts)]
    blocks = [[] for _ in range(parts)]
    for a_ref in (a_own_ref, a_twin_ref):
        with_re = half_nt(t_ref[...], a_ref[0])
        with_im = half_nt(t_ref[...], a_ref[1])
        n_t = parts * group
        with_re = with_re[:n_t] + with_re[n_t:]
        with_im = with_im[:n_t] + with_im[n_t:]
        with_re = with_re.reshape(parts, parts, 2, rows, n_p)
        with_im = with_im.reshape(parts, parts, 2, rows, n_p)
        k_re = with_re[:, :, 0] + with_im[:, :, 1]
        k_im = with_re[:, :, 1] - with_im[:, :, 0]
        for d in range(parts):
            both = jnp.stack([k_re[:, d], k_im[:, d]], axis=1).reshape(-1, n_p)
            for l in range(0, n_p, LANES):
                block = both[:, l : l + LANES]
                if d:
                    tops[d] = jnp.maximum(tops[d], fold_top(block))
                blocks[d].append(block)
    for d in range(parts):
        n_r = blocks[d][0].shape[0]
        if d == 0:
            for l, block in enumerate(blocks[d]):
                outs[d][l * n_r : (l + 1) * n_r, :] = block
            continue
        bound = bound_of(tops[d])
        out, start = outs[d], 0
        if early:
            start = early[d - 1].shape[0]
            out[:start, :] = early[d - 1][...]
        out[start : start + HEAD, :] = spread_head(bound)
        for l, block in enumerate(blocks[d]):
            at = start + HEAD + l * n_r
            out[at : at + n_r, :] = code(block, bound)


def last_body(parts, chunks, rows, where_ref, *refs):
    own, others = refs[:chunks], refs[chunks : chunks + parts - 1]
    outs = refs[chunks + parts - 1 :]
    t = where_ref[0]
    sub = rows * chunks
    n_l = outs[0].shape[2] // LANES
    size = others[0].shape[0] // chunks
    for e in range(chunks):
        n_r = own[e].shape[0] // (2 * n_l)
        start = e * size
        bounds = [x[start : start + 1, :].astype(F32) for x in others]
        for l in range(2 * n_l):
            total = own[e][l * n_r : (l + 1) * n_r, :]
            at = start + HEAD + l * n_r
            for x, bound in zip(others, bounds):
                total = total + decode(x[at : at + n_r, :], bound)
            total = total.reshape(parts, 2, rows, LANES)
            out, lane = outs[l // n_l], l % n_l * LANES
            for i in range(parts):
                at = pl.multiple_of((t ^ i) * sub + e * rows, 8)
                for part in range(2):
                    out[part, pl.ds(at, rows), lane : lane + LANES] = total[i, part]


def turn_body(where_ref, own_ref, twin_ref, out_ref, k_ref):
    core = where_ref[1]
    half = own_ref.shape[1]
    for c, ref in enumerate((own_ref, twin_ref)):
        at = pl.multiple_of((core ^ c) * half, 8)
        k_ref[:, pl.ds(at, half), :] = ref[...]
    for part in range(2):
        out_ref[part] = k_ref[part].T


def after(values, *earlier):
    return lax.optimization_barrier((tuple(values), earlier))[0]


def stationary(n_row, n_col, pair_cc, screened, pair_vv):
    parts, chunks = n_col, CHUNKS
    n_q, width = pair_vv.shape[1:]
    n_p, n_k = pair_cc.shape[1:]
    n_g = screened.shape[1]
    half = n_q // 2
    sub = half // parts
    rows = sub // chunks
    group = parts * 2 * rows
    r, z = lax.axis_index("row"), lax.axis_index("col")
    t, core = r // 2, r % 2
    where = jnp.stack([t, core, t ^ z]).astype(jnp.int32)
    shape = jax.ShapeDtypeStruct
    total_g = 2 * n_g

    def plane(x, i):
        pairs = [(a, a ^ (2 * i)) for a in range(n_row)]
        return lax.ppermute(x, "row", pairs)

    def twin(x):
        return lax.ppermute(x, "row", [(a, a ^ 1) for a in range(n_row)])

    def along(x, d):
        return lax.ppermute(x, "col", [(a, a ^ d) for a in range(parts)])

    def planes(arrays):
        return [arrays[0]] + [plane(arrays[i], i) for i in range(1, parts)]

    def alongs(arrays):
        return [arrays[0]] + [along(arrays[d], d) for d in range(1, parts)]

    def route(arrays, name):
        outs = [shape(a.shape, a.dtype) for a in arrays]
        return call(
            functools.partial(route_body, parts), outs, [], name, [where, *arrays]
        )

    def fetch(x):
        outs, scratch = [shape(x.shape, x.dtype)], [pltpu.SemaphoreType.DMA]
        return call(fetch_body, outs, scratch, "fetch", [where, x], far=1)[0]

    with jax.named_scope("spread_vv"):
        theirs = twin(pair_vv)
        mine = fetch(pair_vv)
        cut = call(
            functools.partial(spread_body, parts, chunks),
            [shape((2 * sub, 2 * width), BF)] * parts,
            [],
            "spread_vv",
            [where, mine, theirs],
        )
        late = after([screened, pair_cc], *cut)
        screened_twin, pair_cc_twin = twin(late[0]), twin(late[1])
        cut = alongs(route(planes(cut), "route_vv"))
        screened_own = fetch(late[0])
        cut = after(cut, screened_own, screened_twin, pair_cc_twin)
        (own,) = call(
            functools.partial(chunk_body, parts, chunks),
            [shape((group * chunks, 2 * width), BF)],
            [],
            "chunk_vv",
            [where, *cut],
        )
    coded = shape((HEAD + total_g // LANES * group, LANES), BF)
    term = shape((HEAD + 2 * n_p // LANES * group, LANES), BF)

    def inner_of(groups):
        n = len(groups)
        return call(
            functools.partial(inner_body, n, chunks, rows),
            [coded] * (n * chunks),
            [
                pltpu.VMEM((n * chunks * group, 2 * width), BF),
                pltpu.VMEM((n * chunks, total_g // LANES, group, LANES), F32),
            ],
            "inner",
            [where, screened_own, screened_twin, *groups],
        )

    summed = pltpu.VMEM((total_g // LANES, group, LANES), F32)

    def deal(arrays):
        outs = [coded, coded, shape((2 * coded.shape[0], LANES), BF)]
        body = functools.partial(deal_body, parts)
        return call(body, outs, [], "deal_inner", [where, *arrays])

    def fold(own, far, got):
        outs = [shape((total_g // LANES, group, LANES), F32), coded]
        body = functools.partial(fold_body, parts)
        return call(body, outs, [summed], "fold_inner", [where, own, far, got])

    def sum_of(kept, got):
        body = functools.partial(sum_body, parts)
        return call(body, [coded], [summed], "sum_inner", [where, kept, got])[0]

    def outer_of(arrays, early):
        n_r = 2 * n_p // LANES * group
        sent = shape(((HEAD + n_r) * (2 if early else 1), LANES), BF)
        return call(
            functools.partial(outer_body, parts, rows, len(early)),
            [shape((n_r, LANES), F32)] + [sent] * (parts - 1),
            [pltpu.VMEM((2 * parts * group, n_k), BF)],
            "outer",
            [where, pair_cc, pair_cc_twin, *arrays, *early],
        )

    with jax.named_scope("inner"):
        groups = planes([own] * parts)
        inner = []
        for batch in BATCHES:
            inner += inner_of([groups[i] for i in batch])
    totals = []
    for e in range(chunks):
        with jax.named_scope("move_inner"):
            mine, far, sent = deal(planes(inner[e::chunks]))
            kept, sent = fold(mine, far, along(sent, 1))
            totals.append(sum_of(kept, along(sent, 2)))
    finals, early = [], []
    with jax.named_scope("outer"):
        for total in totals:
            kept, *early = outer_of(planes([total] * parts), early)
            finals.append(kept)
        finals += [along(x, d) for d, x in enumerate(early, 1)]
    with jax.named_scope("sum_outer"):
        own, theirs = call(
            functools.partial(last_body, parts, chunks, rows),
            [shape((2, half, n_p), F32)] * 2,
            [],
            "sum_outer",
            [where, *finals],
        )
        (result,) = call(
            turn_body,
            [shape((2, n_p, n_q), F32)],
            [pltpu.VMEM((2, n_q, n_p), F32)],
            "turn",
            [where, own, twin(theirs)],
        )
    return result


def power_of_two(n):
    return n > 0 and n & (n - 1) == 0


def solution(mesh):
    placed = (P(None, "row", "col"), P(None, "row", "col"), P(None, "col", "row"))
    n_row, n_col = mesh.shape["row"], mesh.shape["col"]

    def shards(pair_cc, screened, pair_vv):
        n_q, width = pair_vv.shape[1:]
        n_p, n_k = pair_cc.shape[1:]
        n_g = screened.shape[1]
        fits = (
            power_of_two(n_row)
            and power_of_two(n_col)
            and n_row == 2 * n_col
            and n_col == 4
            and n_q % (2 * n_col * CHUNKS * 8) == 0
            and n_q % (2 * n_col * 16) == 0
            and width % LANES == 0
            and n_g == width
            and n_g % 256 == 0
            and n_p % LANES == 0
            and n_k == 2 * width
        )
        if not fits:
            return gathered(pair_cc, screened, pair_vv)
        return stationary(n_row, n_col, pair_cc, screened, pair_vv)

    return jax.shard_map(
        shards, mesh=mesh, in_specs=placed, out_specs=P(None, "row", "col"), check_vma=False
    )
```
